128 devices in a mesh: gz: 64 (over z, y_lo, x, core), col: 2 (over y_hi).
Axes of the slice: x: 4, y: 4 (y_hi: 2, y_lo: 2; y = y_hi * 2 + y_lo), z: 4, core: 2. Of those that a mesh axis runs over, the one named last changes fastest.
Arguments:
- volume: float32 [256, 24, 4096], P('gz', None, 'col'), may hold values from -6 to 6
- images: bfloat16 [256, 264, 2048], P('gz', None, 'col'), may hold values from -96 to 96
- owners: int32 [256], replicated, may hold values from 0 to 255, each once
- subsets: int32 [2, 6], replicated, may hold values from 0 to 255, as said below
- offsets: int32 [64], replicated, may hold values from 0 to 254, as said below
Outputs:
- reconstruction: float32 [256, 24, 4096], P('gz', None, 'col')
The draws below stay inside these ranges and needn't reach their ends.
Inputs may be any that keep to these rules, and one draw needn't show every extreme that they name: `owners`: A permutation: every view number is stored at exactly one position. All view numbers in subsets are distinct; view 0 and view 256 - 1 always appear. offsets[g] - g * 4 lies in 0 .. 2; it is 0 for the first slab and 2 for the last.
All inputs are finite; a program needn't handle non-finite values.
Results may differ from the reference program's by a relative error of at most 0.0003.
Values may be sent and summed in bfloat16 or wider, within the bound.
No kernel may reach another device: no remote copies, remote signals or barrier semaphores. Data moves between devices by JAX's collectives and lax.ppermute only.
A program may use at most 128 MiB of HBM per device.

```python
import jax
import jax.numpy as jnp
from jax import lax

ZS = 4
XW = 24
Y = 4096
SUBSET = 6
SUBSETS = 2
PASSES = 4
MARGIN = 64
U = 2048
NV = 256
NZ = 256
ROWS = 264


def draw_subsets(key, part):
    count = SUBSETS * SUBSET
    shuffled = jax.random.permutation(key, NV - 2).astype(jnp.int32) + 1
    chosen = shuffled[:count - 2]
    listing = jnp.concatenate([chosen, jnp.array([0, NV - 1], jnp.int32)])
    ordering = jax.random.permutation(jax.random.fold_in(key, 7), count)
    return listing[ordering].reshape(SUBSETS, SUBSET).astype(jnp.int32)


def draw_offsets(key, part):
    slab_count = NZ // ZS
    lifts = jax.random.randint(key, (slab_count,), 0, ZS // 2 + 1)
    positions = jnp.arange(slab_count, dtype=jnp.int32)
    lifts = jnp.where(positions == 0, 0, jnp.where(positions == slab_count - 1, ZS // 2, lifts))
    return (positions * ZS + lifts).astype(jnp.int32)


def block_levels(own_key, shape, shards, least, largest):
    level = 1.0
    for axis_at, blocks in shards:
        steps = jax.random.uniform(jax.random.fold_in(jax.random.fold_in(own_key, 6), axis_at), (blocks,), jnp.float32, least / len(shards), largest / len(shards))
        level = level * jnp.repeat(jnp.exp(steps), shape[axis_at] // blocks).reshape((-1,) + (1,) * (len(shape) - 1 - axis_at))
    return level


def noise(stream_key, shape, scale, most, split=(), held_as=jnp.bfloat16):
    loudness = block_levels(stream_key, shape, split, -0.22, 0.18) if split else 1.0
    values = jax.random.normal(stream_key, shape, jnp.float32) * scale * loudness
    return jnp.minimum(jnp.maximum(values, -most), most).astype(held_as)


def setup_inputs(seed: int = 0) -> dict:
    key_of = jax.random.split(jax.random.key(seed), 6)
    volume = noise(key_of[0], (NZ, XW, Y), 1.0, 6.0, ((0, 64), (2, 2)), jnp.float32)
    images = noise(key_of[1], (NV, ROWS, U), 16.0, 96.0, ((0, 64), (2, 2)))
    owners = jax.random.permutation(key_of[2], NV).astype(jnp.int32)
    subsets = draw_subsets(jax.random.fold_in(key_of[5], 71), 0)
    offsets = draw_offsets(jax.random.fold_in(key_of[5], 71), 0)
    return dict(volume=volume, images=images, owners=owners, subsets=subsets, offsets=offsets)


relaxation = 0.8
smooth_step = 0.05
smooth_floor = 0.1

def view_geometry(view, xcount, margin, nviews):
    angles = jnp.pi * view.astype(jnp.float32) / nviews
    across = (2.0 * jnp.arange(xcount, dtype=jnp.float32) - (xcount - 1)) / xcount
    shifted = margin * (0.375 * jnp.cos(angles) + 0.25 * jnp.sin(angles) * across) + margin
    integral = jnp.floor(shifted)
    return (integral.astype(jnp.int32), shifted - integral)

def kernel(fraction):
    half_steps = 0.5 * jnp.arange(128, dtype=jnp.float32)
    columns = jnp.arange(128, dtype=jnp.float32)
    distance = half_steps[None, :, None] + fraction[:, None, None] - columns[None, None, :]
    return jnp.maximum(0.0, 1.0 - jnp.abs(distance))

def project(slices, column_step, weights, margin):
    slab_depth, xcount, length = slices.shape
    block_count = length // 128
    blocks = slices.reshape(slab_depth, xcount, block_count, 128)
    pieces = jnp.einsum('kxby,xyj->xkbj', blocks, weights, precision=lax.Precision.HIGHEST)
    front_half = pieces[..., :64].reshape(xcount, slab_depth, block_count * 64)
    second = pieces[..., 64:].reshape(xcount, slab_depth, block_count * 64)
    joined = jnp.pad(front_half, ((0, 0), (0, 0), (0, 64))) + jnp.pad(second, ((0, 0), (0, 0), (64, 0)))
    padded = jnp.pad(joined, ((0, 0), (0, 0), (2 * margin, 2 * margin)))
    extent = block_count * 64 + 2 * margin

    def moved_row(single, offset_cols):
        return lax.dynamic_slice_in_dim(single, (2 * margin - offset_cols).astype(jnp.int32), extent, axis=1)
    return lax.optimization_barrier(jnp.sum(jax.vmap(moved_row)(padded, column_step), axis=0))

def spread(rows_ext, column_step, weights, length):
    slab_depth = rows_ext.shape[0]
    block_count = length // 128
    padded = jnp.pad(rows_ext, ((0, 0), (0, block_count * 64 + 64)))

    def one_row(offset_cols, weight):
        window = lax.dynamic_slice_in_dim(padded, offset_cols.astype(jnp.int32), block_count * 64 + 64, axis=1)
        lower = window[:, :block_count * 64].reshape(slab_depth, block_count, 64)
        upper = window[:, 64:].reshape(slab_depth, block_count, 64)
        stacked = jnp.concatenate([lower, upper], axis=2)
        result = jnp.einsum('kbj,yj->kby', stacked, weight, precision=lax.Precision.HIGHEST)
        return result.reshape(slab_depth, length)
    return jax.vmap(one_row, out_axes=1)(column_step, weights)

def forward_diff(values, direction):
    count = values.shape[direction]
    following = jnp.concatenate([lax.slice_in_dim(values, 1, count, axis=direction), jnp.zeros_like(lax.slice_in_dim(values, 0, 1, axis=direction))], axis=direction)
    return following - values

def behind(values, direction):
    count = values.shape[direction]
    return jnp.concatenate([jnp.zeros_like(lax.slice_in_dim(values, 0, 1, axis=direction)), lax.slice_in_dim(values, 0, count - 1, axis=direction)], axis=direction)

def smooth_pass(padded, inside):
    differences = [forward_diff(padded, direction) for direction in range(3)]
    magnitude = jnp.sqrt(differences[0] * differences[0] + differences[1] * differences[1] + differences[2] * differences[2] + smooth_floor)
    fluxes = [item_diff / magnitude * inside for item_diff in differences]
    gradient = behind(fluxes[0], 0) - fluxes[0] + (behind(fluxes[1], 1) - fluxes[1]) + (behind(fluxes[2], 2) - fluxes[2])
    return (padded - smooth_step * gradient) * inside

def reference(volume, images, owners, subsets, offsets):
    slice_ids = jnp.arange(NZ, dtype=jnp.int32)
    rows_all = jnp.arange(ROWS, dtype=jnp.float32)
    centers = offsets[slice_ids // ZS].astype(jnp.float32) + 1.5 * (slice_ids % ZS).astype(jnp.float32) + 0.25
    row_weight = jnp.maximum(0.0, 1.0 - jnp.abs(centers[None, :] - rows_all[:, None]))
    row_total = lax.optimization_barrier(jnp.sum(row_weight, axis=1))
    stored = jnp.arange(NV, dtype=jnp.int32)
    unit_slice = jnp.ones((1, XW, Y), jnp.float32)
    current = volume
    for subset_index in range(SUBSETS):
        stacked = jnp.concatenate([current, unit_slice], axis=0)

        def one_view(running, view):
            column_step, fraction = view_geometry(view, XW, MARGIN, NV)
            weights = kernel(fraction)
            extended = project(stacked, column_step, weights, MARGIN)
            forward = extended[:NZ, MARGIN:MARGIN + U]
            onesum = extended[NZ, MARGIN:MARGIN + U]
            predicted = jnp.dot(row_weight, forward, precision=lax.Precision.HIGHEST, preferred_element_type=jnp.float32)
            raysum = row_total[:, None] * onesum[None, :]
            position = jnp.sum(jnp.where(owners == view, stored, 0)).astype(jnp.int32)
            measured = lax.dynamic_index_in_dim(images, position, 0, keepdims=False).astype(jnp.float32)
            residual = (measured - predicted) / jnp.maximum(raysum, 1.0)
            backward = jnp.dot(row_weight.T, residual, precision=lax.Precision.HIGHEST, preferred_element_type=jnp.float32)
            backward = jnp.pad(backward, ((0, 0), (MARGIN, MARGIN)))
            return (running + spread(backward, column_step, weights, Y), None)
        update, _ = lax.scan(one_view, jnp.zeros((NZ, XW, Y), jnp.float32), subsets[subset_index])
        current = current + relaxation / SUBSET * update
        inside = jnp.pad(jnp.ones((NZ, XW, Y), jnp.float32), 1)
        for pass_index in range(PASSES):
            current = smooth_pass(jnp.pad(current, 1), inside)[1:-1, 1:-1, 1:-1]
    return current
```

```python
import functools

import jax
import jax.numpy as jnp
from jax import lax
from jax.experimental import pallas as pl
from jax.experimental.pallas import tpu as pltpu
from jax.sharding import PartitionSpec as P

SUBSET = 6
SUBSETS = 2
PASSES = 4
MARGIN = 64

relaxation = 0.8
smooth_step = 0.05
smooth_floor = 0.1

ZS = 4
XW = 24
TILES = 9
WIDE = TILES * 128
WINDOW = 8
HIGHEST = lax.Precision.HIGHEST
PARAMS = pltpu.CompilerParams(vmem_limit_bytes=48 * 1024 * 1024)
F32 = jnp.float32


def view_geometry(view, xcount, margin, nviews):
    angles = jnp.pi * view.astype(jnp.float32) / nviews
    across = (2.0 * jnp.arange(xcount, dtype=jnp.float32) - (xcount - 1)) / xcount
    shifted = margin * (
        0.375 * jnp.cos(angles)[:, None] + 0.25 * jnp.sin(angles)[:, None] * across[None, :]
    ) + margin
    integral = jnp.floor(shifted)
    return (integral.astype(jnp.int32), shifted - integral)


def iota2(dim, rows=8):
    return lax.broadcasted_iota(jnp.int32, (rows, 128), dim)


def taps(fraction):
    reach = jnp.where(iota2(0) >= ZS, 0.5, 0.0) + fraction
    return (
        jnp.maximum(0.0, 1.0 - reach),
        1.0 - jnp.abs(reach - 1.0),
        jnp.maximum(0.0, reach - 1.0),
    )


def row_weights(shift, transposed):
    i = iota2(0)
    z = i if transposed else i - shift
    centers = 1.5 * z.astype(F32) + 0.25
    rows = (z + shift).astype(F32)
    weight = jnp.maximum(0.0, 1.0 - jnp.abs(centers - rows))
    return jnp.where((z >= 0) & (z < ZS), weight, 0.0)


def split_matrix(joined):
    r = lax.broadcasted_iota(jnp.int32, (256, 256), 0)
    c = lax.broadcasted_iota(jnp.int32, (256, 256), 1)
    if joined:
        r, c = c, r
    return (r == jnp.where(c < 128, 2 * c, 2 * (c - 128) + 1)).astype(F32)


def project(state, steps, fractions, base, rows_ref, rows16_ref):
    lane = iota2(1)
    weights = [row_weights(shift, False) for shift in range(3)]
    zero = jnp.zeros((8, 128), F32)
    pair = []
    for v in range(SUBSET):

        def one_x(x, sums):
            at = (base + v) * XW + x
            step = steps[at]
            coef = taps(fractions[at])
            here = pl.ds(pl.multiple_of(8 * x, 8), 8)
            turned = [pltpu.roll(state[j, here, :], step, 1) for j in range(TILES)]
            mask = lane >= step
            before = [zero] + turned
            after = turned + [zero]
            moved = [jnp.where(mask, after[j], before[j]) for j in range(TILES + 1)]
            return tuple(
                sums[k * (TILES + 1) + j] + coef[k] * moved[j]
                for k in range(3)
                for j in range(TILES + 1)
            )

        sums = lax.fori_loop(0, XW, one_x, (zero,) * (3 * (TILES + 1)), unroll=2)
        frame = []
        once = [zero] + [pltpu.roll(sums[TILES + 1 + j], 1, 1) for j in range(TILES + 1)]
        twice = [zero] + [pltpu.roll(sums[2 * TILES + 2 + j], 2, 1) for j in range(TILES + 1)]
        for j in range(TILES + 1):
            total = (
                sums[j]
                + jnp.where(lane >= 1, once[j + 1], once[j])
                + jnp.where(lane >= 2, twice[j + 1], twice[j])
            )
            total = total + pltpu.roll(total, 4, 0)
            rows = (
                weights[0] * total
                + weights[1] * pltpu.roll(total, 1, 0)
                + weights[2] * pltpu.roll(total, 2, 0)
            )
            frame.append(pltpu.roll(rows, 64, 1))
        out = [jnp.where(lane < 64, frame[j], frame[j + 1]) for j in range(TILES)]
        for j in range(TILES):
            rows_ref[8 * v : 8 * v + 8, 128 * j : 128 * j + 128] = out[j]
        pair.append(out)
        if v % 2:
            for j in range(TILES):
                both = jnp.concatenate([pair[v - 1][j], pair[v][j]], axis=0)
                rows16_ref[8 * v - 8 : 8 * v + 8, 128 * j : 128 * j + 128] = both.astype(
                    jnp.bfloat16
                )


def pack_kernel(place, first, second, edge_first, edge_second, out, held):
    column = place[0]
    for slot, (image, edge) in enumerate(((first, edge_first), (second, edge_second))):

        @pl.when(column == 0)
        def _():
            held[slot, :, :1024] = image[0].astype(F32)
            held[slot, :, 1024:] = edge[0].astype(F32)

        @pl.when(column == 1)
        def _():
            held[slot, :, 128:] = image[0].astype(F32)
            held[slot, :, :128] = edge[0].astype(F32)

    row = lax.broadcasted_iota(jnp.int32, (8, WIDE), 0)

    def two_slabs(i, carry):
        low, high = [], []
        for slot in range(2):
            a = held[slot, pl.ds(pl.multiple_of(8 * i, 8), 8), :]
            b = held[slot, pl.ds(pl.multiple_of(8 * i + 8, 8), 8), :]
            low.append(a)
            high.append(jnp.where(row < 4, pltpu.roll(a, 4, 0), pltpu.roll(b, 4, 0)))
        out[2 * i] = jnp.concatenate(low, axis=0).astype(jnp.bfloat16)
        out[2 * i + 1] = jnp.concatenate(high, axis=0).astype(jnp.bfloat16)
        return carry

    lax.fori_loop(0, out.shape[0] // 2, two_slabs, 0)


def pack(place, slots, images, edges, slab_count):
    rows = images.shape[1]
    spec = pltpu.PrefetchScalarGridSpec(
        num_scalar_prefetch=2,
        grid=(1,),
        in_specs=[
            pl.BlockSpec((1, rows, 1024), lambda i, p, s: (s[0], 0, 0)),
            pl.BlockSpec((1, rows, 1024), lambda i, p, s: (s[1], 0, 0)),
            pl.BlockSpec((1, rows, 128), lambda i, p, s: (s[0], 0, 0)),
            pl.BlockSpec((1, rows, 128), lambda i, p, s: (s[1], 0, 0)),
        ],
        out_specs=pl.BlockSpec((slab_count, 16, WIDE), lambda i, p, s: (0, 0, 0)),
        scratch_shapes=[pltpu.VMEM((2, rows, WIDE), F32)],
    )

    def kernel(p, s, *refs):
        pack_kernel(p, *refs)

    return pl.pallas_call(
        kernel,
        grid_spec=spec,
        out_shape=jax.ShapeDtypeStruct((slab_count, 16, WIDE), jnp.bfloat16),
        compiler_params=PARAMS,
        name="pack_images",
    )(place, slots, images, images, edges, edges)


def start_kernel(place, steps, fractions, volume, edge, state, rows_ref, rows16_ref):
    column = place[0]
    matrix = split_matrix(False)

    def put(pixels, tile):
        halves = jnp.dot(
            pixels.reshape(ZS * XW, 256), matrix, precision=HIGHEST, preferred_element_type=F32
        )
        for z in range(ZS):
            for p in range(2):
                state[tile, pl.ds(4 * p + z, XW, stride=8), :] = halves[
                    XW * z : XW * z + XW, 128 * p : 128 * p + 128
                ]

    for j in range(TILES - 1):
        put(volume[:, :, 256 * j : 256 * j + 256], j + column)
    put(edge[...], (TILES - 1) * (1 - column))
    project(state, steps, fractions, 0, rows_ref, rows16_ref)


def scalar_call(kernel, scalars, arrays, out_shape, scratch, name):
    vmem = pl.BlockSpec(memory_space=pltpu.VMEM)
    smem = pl.BlockSpec(memory_space=pltpu.SMEM)
    single = not isinstance(out_shape, (list, tuple))
    return pl.pallas_call(
        kernel,
        in_specs=[smem] * len(scalars) + [vmem] * len(arrays),
        out_specs=vmem if single else [vmem] * len(out_shape),
        out_shape=out_shape,
        scratch_shapes=scratch,
        compiler_params=PARAMS,
        name=name,
    )(*scalars, *arrays)


ROWS_OUT = (
    jax.ShapeDtypeStruct((TILES, 8 * XW, 128), F32),
    jax.ShapeDtypeStruct((8 * SUBSET, WIDE), F32),
    jax.ShapeDtypeStruct((8 * SUBSET, WIDE), jnp.bfloat16),
)
SLAB = (ZS, TILES, 2, XW, 128)


def update_kernel(base, place, owner, rank, steps, fractions, *refs):
    images, extra = refs[:SUBSET], refs[SUBSET : 2 * SUBSET]
    state, own, before, after, out, held, moved_state = refs[2 * SUBSET :]
    column, to_before, to_after = place[0], place[1], place[2]
    has_before, has_after, lift = place[3], place[4], place[5]
    lane, sub = iota2(1), iota2(0)
    zero = jnp.zeros((8, 128), F32)
    totals = row_weights(0, False) + row_weights(1, False) + row_weights(2, False)

    def shifted_rows(value, by):
        row = sub + by
        turned = pltpu.roll(value, lax.rem(16 - by, 8), 0)
        return jnp.where((row >= 0) & (row < 8), turned, 0.0)

    row_total = (
        totals
        + shifted_rows(totals, to_before) * has_before.astype(F32)
        + shifted_rows(totals, to_after) * has_after.astype(F32)
    )
    inner = jnp.maximum(row_total * float(2 * XW), 1.0)
    back_weights = [row_weights(shift, True) for shift in range(3)]
    edge_tile = column * (TILES - 1)
    edge_column = lane + column * (2048 - 128)

    for v in range(SUBSET):

        def one_x(x, total):
            at = (base + v) * XW + x
            fraction = fractions[at]
            pixel = edge_column - (steps[at] - MARGIN)
            weights = (
                jnp.maximum(0.0, 1.0 - fraction) + jnp.maximum(0.0, 0.5 - fraction),
                1.0 - jnp.abs(fraction - 1.0) + (1.0 - jnp.abs(fraction - 0.5)),
                jnp.maximum(0.0, fraction - 0.5),
            )
            for k in range(3):
                inside = (pixel - k >= 0) & (pixel - k < 2048)
                total = total + jnp.where(inside, weights[k], 0.0)
            return total

        edge_sum = lax.fori_loop(0, XW, one_x, zero, unroll=4)
        outer = jnp.maximum(row_total * edge_sum, 1.0)
        slot = rank[base + v]
        take = 8 * lax.rem(slot, 2) + lift
        later = (slot >= 2)
        turned = []
        if v % 2 == 0:
            pair_before = before[8 * v : 8 * v + 16, :].astype(F32)
            pair_after = after[8 * v : 8 * v + 16, :].astype(F32)
        low = 8 * (v % 2)
        image = jnp.where(later, extra[v][0].astype(F32), images[v][0].astype(F32))
        image = pltpu.roll(image, lax.rem(16 - take, 16), 0)[:8]
        for j in range(TILES):
            cols = slice(128 * j, 128 * j + 128)
            predicted = (
                own[8 * v : 8 * v + 8, cols]
                + shifted_rows(pair_before[low : low + 8, cols], to_before)
                + shifted_rows(pair_after[low : low + 8, cols], to_after)
            )
            raysum = inner
            if j == 0 or j == TILES - 1:
                raysum = jnp.where(edge_tile == j, outer, inner)
            residual = (image[:, cols] - predicted) / raysum
            mixed = back_weights[0] * residual
            for shift in (1, 2):
                mixed = mixed + back_weights[shift] * pltpu.roll(residual, 8 - shift, 0)
            mixed = mixed + pltpu.roll(mixed, 4, 0)
            turned.append(pltpu.roll(mixed, 64, 1))
        frame = [
            jnp.where(lane < 64, a, b) for a, b in zip([zero] + turned, turned + [zero])
        ]
        for shift in range(3):
            if shift == 0:
                rows = frame
            else:
                back = [pltpu.roll(tile, 128 - shift, 1) for tile in frame] + [zero]
                rows = [
                    jnp.where(lane < 128 - shift, back[j], back[j + 1])
                    for j in range(TILES + 1)
                ]
            for j in range(TILES + 1):
                held[v, shift, j] = rows[j]

    def back_x(x, carry):
        here = pl.ds(pl.multiple_of(8 * x, 8), 8)
        totals_x = [zero] * TILES
        for v in range(SUBSET):
            at = (base + v) * XW + x
            step = steps[at]
            coef = taps(fractions[at])
            turned = []
            for j in range(TILES + 1):
                mix = (
                    coef[0] * held[v, 0, j] + coef[1] * held[v, 1, j] + coef[2] * held[v, 2, j]
                )
                turned.append(pltpu.roll(mix, 128 - step, 1))
            mask = lane < 128 - step
            totals_x = [
                totals_x[j] + jnp.where(mask, turned[j], turned[j + 1]) for j in range(TILES)
            ]
        for j in range(TILES):
            moved_state[j, here, :] = state[j, here, :] + (relaxation / SUBSET) * totals_x[j]
        return carry

    lax.fori_loop(0, XW, back_x, 0)
    for j in range(TILES):
        for z in range(ZS):
            for p in range(2):
                out[z, j, p] = moved_state[j, pl.ds(4 * p + z, XW, stride=8), :]


def update(subset, place, owner, rank, steps, fractions, recv, extra, state, own, before, after):
    base = subset * SUBSET

    def of_view(v):
        return pl.BlockSpec(
            (1, 16, WIDE), lambda i, place, owner, rank, steps, fr: (owner[base + v], 0, 0)
        )

    def whole(array):
        rank_of = array.ndim
        return pl.BlockSpec(array.shape, lambda i, *scalars: (0,) * rank_of)

    spec = pltpu.PrefetchScalarGridSpec(
        num_scalar_prefetch=5,
        grid=(1,),
        in_specs=[of_view(v) for v in range(SUBSET)] * 2
        + [whole(a) for a in (state, own, before, after)],
        out_specs=pl.BlockSpec(SLAB, lambda i, *scalars: (0,) * 5),
        scratch_shapes=[
            pltpu.VMEM((SUBSET, 3, TILES + 1, 8, 128), F32),
            pltpu.VMEM((TILES, 8 * XW, 128), F32),
        ],
    )
    return pl.pallas_call(
        functools.partial(update_kernel, base),
        grid_spec=spec,
        out_shape=jax.ShapeDtypeStruct(SLAB, F32),
        compiler_params=PARAMS,
        name="residual_back",
    )(
        place, owner, rank, steps, fractions,
        *([recv] * SUBSET), *([extra] * SUBSET), state, own, before, after,
    )


def smooth(own, before, after, buffers, along, in_before, in_after, store):
    sources = (before, own, after)
    row24 = lax.broadcasted_iota(jnp.int32, (XW, 128), 0)
    lane24 = lax.broadcasted_iota(jnp.int32, (XW, 128), 1)
    zero = jnp.zeros((XW, 128), F32)
    for index in range(PASSES):
        low, high = 1 + index, 10 - index
        last = index == PASSES - 1
        target = buffers[index % 2]
        source = buffers[(index + 1) % 2]

        def load(z, j, parity, index=index, source=source):
            if index == 0:
                return sources[z // ZS][z % ZS, j, parity]
            return source[z, j, parity]

        for z in range(low, high + 1):
            along[z] = zero

        def one_tile(j, carry, low=low, high=high, last=last, target=target, load=load):
            following = jnp.minimum(j + 1, TILES - 1)
            has_following = j < TILES - 1
            current = [load(low - 1, j, p) for p in range(2)]
            flux_before = None
            for z in range(low - 1, high + 1):
                above = [load(z + 1, j, p) for p in range(2)]
                beside = jnp.where(has_following, load(z, following, 0), 0.0)
                next_even = pltpu.roll(
                    jnp.where(lane24 == 0, beside, current[0]), 127, 1
                )
                ahead = [current[1], next_even]
                fluxes = []
                for p in range(2):
                    c = current[p]
                    dz = above[p] - c
                    dx = jnp.where(row24 < XW - 1, pltpu.roll(c, XW - 1, 0), 0.0) - c
                    dy = ahead[p] - c
                    scale = lax.rsqrt(dz * dz + dx * dx + dy * dy + smooth_floor)
                    fluxes.append((dz * scale, dx * scale, dy * scale))
                flux_z = [fluxes[p][0] for p in range(2)]
                if z < ZS:
                    flux_z = [f * in_before for f in flux_z]
                if z >= low:
                    turned = pltpu.roll(fluxes[1][2], 1, 1)
                    behind_even = jnp.where(lane24 == 0, along[z], turned)
                    along[z] = turned
                    behind = [behind_even, fluxes[0][2]]
                    for p in range(2):
                        flux_x = fluxes[p][1]
                        back_x = jnp.where(row24 > 0, pltpu.roll(flux_x, 1, 0), 0.0)
                        gradient = (
                            (flux_before[p] - fluxes[p][0])
                            + (back_x - flux_x)
                            + (behind[p] - fluxes[p][2])
                        )
                        fresh = current[p] - smooth_step * gradient
                        if z < ZS:
                            fresh = fresh * in_before
                        if z >= 2 * ZS:
                            fresh = fresh * in_after
                        if last:
                            store(z - ZS, j, p, fresh)
                        else:
                            target[z, j, p] = fresh
                flux_before = flux_z
                current = above
            return carry

        lax.fori_loop(0, TILES, one_tile, 0)


SMOOTH_SCRATCH = [
    pltpu.VMEM((3 * ZS, TILES, 2, XW, 128), F32),
    pltpu.VMEM((3 * ZS, TILES, 2, XW, 128), F32),
    pltpu.VMEM((3 * ZS, XW, 128), F32),
]


def smooth_project_kernel(
    place, steps, fractions, own, before, after, state, rows_ref, rows16_ref, one, two, along
):
    def store(z, j, p, value):
        state[j, pl.ds(4 * p + z, XW, stride=8), :] = value

    smooth(
        own, before, after, (one, two), along,
        place[3].astype(F32), place[4].astype(F32), store,
    )
    project(state, steps, fractions, SUBSET, rows_ref, rows16_ref)


def smooth_end_kernel(place, own, before, after, out, one, two, along):
    def store(z, j, p, value):
        two[z, j, p] = value

    smooth(
        own, before, after, (one, two), along,
        place[3].astype(F32), place[4].astype(F32), store,
    )
    matrix = split_matrix(True)
    column = place[0]
    for j in range(TILES - 1):
        pixels = jnp.concatenate(
            [
                jnp.concatenate([two[z, j + column, 0], two[z, j + column, 1]], axis=1)
                for z in range(ZS)
            ],
            axis=0,
        )
        joined = jnp.dot(pixels, matrix, precision=HIGHEST, preferred_element_type=F32)
        out[:, :, 256 * j : 256 * j + 256] = joined.reshape(ZS, XW, 256)


def to_next(value):
    count = lax.axis_size("gz")
    return lax.ppermute(value, "gz", [(i, i + 1) for i in range(count - 1)])


def to_before(value):
    count = lax.axis_size("gz")
    return lax.ppermute(value, "gz", [(i + 1, i) for i in range(count - 1)])


def swap_halves(value):
    return lax.ppermute(value, "col", [(0, 1), (1, 0)])


def body(volume, images, owners, subsets, offsets):
    slab_count = lax.axis_size("gz")
    slab = lax.axis_index("gz")
    column = lax.axis_index("col")
    stored = images.shape[0]
    nviews = owners.shape[0]

    edge = swap_halves(jnp.where(column == 0, volume[:, :, -256:], volume[:, :, :256]))
    image_edge = swap_halves(jnp.where(column == 0, images[:, :, -128:], images[:, :, :128]))

    views = subsets.reshape(-1)
    positions = jnp.sum(
        jnp.where(
            owners[None, :] == views[:, None], jnp.arange(nviews, dtype=jnp.int32)[None, :], 0
        ),
        axis=1,
    )
    owner = positions // stored
    count = SUBSETS * SUBSET
    order = jnp.arange(count)
    rank = jnp.sum(
        ((owner[None, :] == owner[:, None]) & (order[None, :] < order[:, None])).astype(jnp.int32),
        axis=1,
    )
    slots = jnp.sum(
        jnp.where(
            (owner[None, :] == slab) & (rank[None, :] == jnp.arange(4)[:, None]),
            (positions % stored)[None, :],
            0,
        ),
        axis=1,
    )
    steps, fractions = view_geometry(views, XW, MARGIN, nviews)
    steps, fractions = steps.reshape(-1), fractions.reshape(-1)

    own_start = offsets[slab]
    before_start = offsets[jnp.maximum(slab - 1, 0)]
    next_start = offsets[jnp.minimum(slab + 1, slab_count - 1)]
    place = jnp.stack(
        [
            column,
            own_start - before_start,
            own_start - next_start,
            (slab > 0).astype(jnp.int32),
            (slab < slab_count - 1).astype(jnp.int32),
            own_start - slab * ZS,
        ]
    ).astype(jnp.int32)

    def fetched(two_slots):
        packed = pack(place, two_slots, images, image_edge, slab_count)
        return lax.all_to_all(packed, "gz", 0, 0)

    recv = fetched(slots[:2])
    extra = lax.cond(
        jnp.max(rank) >= 2,
        lambda: fetched(slots[2:]),
        lambda: jnp.zeros((slab_count, 16, WIDE), jnp.bfloat16),
    )

    state, rows, rows16 = scalar_call(
        start_kernel, (place, steps, fractions), (volume, edge), ROWS_OUT, [], "split_project"
    )
    for subset in range(SUBSETS):
        fresh = update(
            subset, place, owner, rank, steps, fractions, recv, extra,
            state, rows, to_next(rows16), to_before(rows16),
        )
        around = (fresh, to_next(fresh), to_before(fresh))
        if subset < SUBSETS - 1:
            state, rows, rows16 = scalar_call(
                smooth_project_kernel, (place, steps, fractions), around, ROWS_OUT,
                SMOOTH_SCRATCH, "smooth_project",
            )
    return scalar_call(
        smooth_end_kernel, (place,), around,
        jax.ShapeDtypeStruct(volume.shape, F32), SMOOTH_SCRATCH, "smooth_join",
    )


def solution(mesh):
    in_specs = (P("gz", None, "col"), P("gz", None, "col"), P(), P(), P())
    out_specs = P("gz", None, "col")
    return jax.shard_map(body, mesh=mesh, in_specs=in_specs, out_specs=out_specs, check_vma=False)
```

```python
import functools

import jax
import jax.numpy as jnp
from jax import lax
from jax.experimental import pallas as pl
from jax.experimental.pallas import tpu as pltpu
from jax.sharding import PartitionSpec as P

SUBSET = 6
SUBSETS = 2
PASSES = 4
MARGIN = 64

relaxation = 0.8
smooth_step = 0.05
smooth_floor = 0.1

ZS = 4
XW = 24
TILES = 9
WIDE = TILES * 128
USED = 6
PACKED = 112
HIGHEST = lax.Precision.HIGHEST
PARAMS = pltpu.CompilerParams(vmem_limit_bytes=48 * 1024 * 1024)
F32 = jnp.float32
PROJECT_UNROLL = 24
BACK_UNROLL = 8


def view_geometry(view, xcount, margin, nviews):
    angles = jnp.pi * view.astype(jnp.float32) / nviews
    across = (2.0 * jnp.arange(xcount, dtype=jnp.float32) - (xcount - 1)) / xcount
    shifted = margin * (
        0.375 * jnp.cos(angles)[:, None] + 0.25 * jnp.sin(angles)[:, None] * across[None, :]
    ) + margin
    integral = jnp.floor(shifted)
    return (integral.astype(jnp.int32), shifted - integral)


def iota2(dim, rows=8):
    return lax.broadcasted_iota(jnp.int32, (rows, 128), dim)


def taps(fraction):
    reach = jnp.where(iota2(0) >= ZS, 0.5, 0.0) + fraction
    return (
        jnp.maximum(0.0, 1.0 - reach),
        1.0 - jnp.abs(reach - 1.0),
        jnp.maximum(0.0, reach - 1.0),
    )


def row_weights(shift, transposed):
    i = iota2(0)
    z = i if transposed else i - shift
    centers = 1.5 * z.astype(F32) + 0.25
    rows = (z + shift).astype(F32)
    weight = jnp.maximum(0.0, 1.0 - jnp.abs(centers - rows))
    return jnp.where((z >= 0) & (z < ZS), weight, 0.0)


def split_matrix(joined):
    r = lax.broadcasted_iota(jnp.int32, (256, 256), 0)
    c = lax.broadcasted_iota(jnp.int32, (256, 256), 1)
    if joined:
        r, c = c, r
    return (r == jnp.where(c < 128, 2 * c, 2 * (c - 128) + 1)).astype(F32)


def project(state, steps, fractions, base, rows_ref, rows16_ref):
    lane = iota2(1)
    weights = [row_weights(shift, False) for shift in range(3)]
    zero = jnp.zeros((8, 128), F32)
    pair = []
    for v in range(SUBSET):

        def one_x(x, sums):
            at = (base + v) * XW + x
            step = steps[at]
            coef = taps(fractions[at])
            here = pl.ds(pl.multiple_of(8 * x, 8), 8)
            turned = [pltpu.roll(state[j, here, :], step, 1) for j in range(TILES)]
            mask = lane >= step
            before = [zero] + turned
            after = turned + [zero]
            moved = [jnp.where(mask, after[j], before[j]) for j in range(TILES + 1)]
            return tuple(
                sums[k * (TILES + 1) + j] + coef[k] * moved[j]
                for k in range(3)
                for j in range(TILES + 1)
            )

        sums = lax.fori_loop(0, XW, one_x, (zero,) * (3 * (TILES + 1)), unroll=PROJECT_UNROLL)
        frame = []
        once = [zero] + [pltpu.roll(sums[TILES + 1 + j], 1, 1) for j in range(TILES + 1)]
        twice = [zero] + [pltpu.roll(sums[2 * TILES + 2 + j], 2, 1) for j in range(TILES + 1)]
        for j in range(TILES + 1):
            total = (
                sums[j]
                + jnp.where(lane >= 1, once[j + 1], once[j])
                + jnp.where(lane >= 2, twice[j + 1], twice[j])
            )
            total = total + pltpu.roll(total, 4, 0)
            rows = (
                weights[0] * total
                + weights[1] * pltpu.roll(total, 1, 0)
                + weights[2] * pltpu.roll(total, 2, 0)
            )
            frame.append(pltpu.roll(rows, 64, 1))
        out = [jnp.where(lane < 64, frame[j], frame[j + 1]) for j in range(TILES)]
        for j in range(TILES):
            rows_ref[8 * v : 8 * v + 8, 128 * j : 128 * j + 128] = out[j]
        pair.append(out)
        if v % 2:
            for j in range(TILES):
                both = jnp.concatenate([pair[v - 1][j], pair[v][j]], axis=0)
                rows16_ref[8 * v - 8 : 8 * v + 8, 128 * j : 128 * j + 128] = both.astype(
                    jnp.bfloat16
                )


def pack_kernel(first_slot, owners, subsets, offsets, images, edges, out, got, got_edge, held, sems):
    slab, column = lax.axis_index("gz"), lax.axis_index("col")
    stored = images.shape[0]
    count = subsets.shape[0]
    found = jnp.int32(0)
    slots = [jnp.int32(0), jnp.int32(0)]
    for i in range(stored):
        view = owners[stored * slab + i]
        hits = jnp.int32(0)
        for k in range(count):
            hits = hits + (subsets[k] == view).astype(jnp.int32)
        for slot in range(2):
            slots[slot] = jnp.where((hits > 0) & (found == first_slot + slot), i, slots[slot])
        found = found + hits
    copies = []
    for slot in range(2):
        copies.append(pltpu.make_async_copy(images.at[slots[slot]], got.at[slot], sems.at[slot]))
        copies.append(
            pltpu.make_async_copy(edges.at[slots[slot]], got_edge.at[slot], sems.at[2 + slot])
        )
    for copy in copies:
        copy.start()
    for copy in copies:
        copy.wait()
    for slot in range(2):
        for j in range(TILES - 1):
            held[slot, j + column] = got[slot, :, 128 * j : 128 * j + 128].astype(F32)
        held[slot, (TILES - 1) * (1 - column)] = got_edge[slot].astype(F32)

    row = iota2(0)

    def one_slab(i, carry):
        window = pl.ds(offsets[i], 8)
        parts = []
        for j in range(TILES):
            b = pltpu.roll(held[1, j, window, :], 6, 0)
            a = jnp.where(row < USED, held[0, j, window, :], b)
            if j % 2 == 0:
                parts += [a, b]
            else:
                middle = pltpu.roll(a, 4, 0)
                parts[-1] = jnp.where(row < 4, parts[-1], middle)
                parts.append(jnp.where(row < 4, middle, pltpu.roll(b, 4, 0)))
        out[i] = jnp.concatenate(parts, axis=0).astype(jnp.bfloat16)
        return carry

    lax.fori_loop(0, out.shape[0], one_slab, 0, unroll=2)


def pack(first_slot, owners, subsets, offsets, images, edges):
    rows = images.shape[1]
    smem = pl.BlockSpec(memory_space=pltpu.SMEM)
    hbm = pl.BlockSpec(memory_space=pl.ANY)
    return pl.pallas_call(
        functools.partial(pack_kernel, first_slot),
        in_specs=[smem] * 3 + [hbm] * 2,
        out_specs=pl.BlockSpec(memory_space=pltpu.VMEM),
        out_shape=jax.ShapeDtypeStruct((offsets.shape[0], PACKED, 128), jnp.bfloat16),
        scratch_shapes=[
            pltpu.VMEM((2, rows, 1024), jnp.bfloat16),
            pltpu.VMEM((2, rows, 128), jnp.bfloat16),
            pltpu.VMEM((2, TILES, rows, 128), F32),
            pltpu.SemaphoreType.DMA((4,)),
        ],
        compiler_params=PARAMS,
        name="pack_images",
    )(owners, subsets, offsets, images, edges)


def start_kernel(place, steps, fractions, volume, edge, state, rows_ref, rows16_ref):
    column = place[0]
    matrix = split_matrix(False)

    def put(pixels, tile):
        halves = jnp.dot(
            pixels.reshape(ZS * XW, 256), matrix, precision=HIGHEST, preferred_element_type=F32
        )
        for z in range(ZS):
            for p in range(2):
                state[tile, pl.ds(4 * p + z, XW, stride=8), :] = halves[
                    XW * z : XW * z + XW, 128 * p : 128 * p + 128
                ]

    for j in range(TILES - 1):
        put(volume[:, :, 256 * j : 256 * j + 256], j + column)
    put(edge[...], (TILES - 1) * (1 - column))
    project(state, steps, fractions, 0, rows_ref, rows16_ref)


def scalar_call(kernel, scalars, arrays, out_shape, scratch, name):
    vmem = pl.BlockSpec(memory_space=pltpu.VMEM)
    smem = pl.BlockSpec(memory_space=pltpu.SMEM)
    single = not isinstance(out_shape, (list, tuple))
    return pl.pallas_call(
        kernel,
        in_specs=[smem] * len(scalars) + [vmem] * len(arrays),
        out_specs=vmem if single else [vmem] * len(out_shape),
        out_shape=out_shape,
        scratch_shapes=scratch,
        compiler_params=PARAMS,
        name=name,
    )(*scalars, *arrays)


ROWS_OUT = (
    jax.ShapeDtypeStruct((TILES, 8 * XW, 128), F32),
    jax.ShapeDtypeStruct((8 * SUBSET, WIDE), F32),
    jax.ShapeDtypeStruct((8 * SUBSET, WIDE), jnp.bfloat16),
)
HALO = jax.ShapeDtypeStruct((ZS + 1, TILES, 2 * XW, 128), jnp.bfloat16)
SLAB_OUT = (jax.ShapeDtypeStruct((ZS, TILES, 2, XW, 128), F32), HALO, HALO)


def update_kernel(base, place, owner, rank, steps, fractions, *refs):
    images, extra = refs[:SUBSET], refs[SUBSET : 2 * SUBSET]
    state, own, before, after, out, out_before, out_after, held, moved_state, rows_of = refs[
        2 * SUBSET :
    ]
    column, to_before, to_after = place[0], place[1], place[2]
    has_before, has_after = place[3], place[4]
    lane, sub = iota2(1), iota2(0)
    zero = jnp.zeros((8, 128), F32)
    totals = row_weights(0, False) + row_weights(1, False) + row_weights(2, False)

    def shifted_rows(value, by):
        row = sub + by
        turned = pltpu.roll(value, lax.rem(16 - by, 8), 0)
        return jnp.where((row >= 0) & (row < 8), turned, 0.0)

    row_total = (
        totals
        + shifted_rows(totals, to_before) * has_before.astype(F32)
        + shifted_rows(totals, to_after) * has_after.astype(F32)
    )
    inner = jnp.maximum(row_total * float(2 * XW), 1.0)
    back_weights = [row_weights(shift, True) for shift in range(3)]
    edge_tile = column * (TILES - 1)
    edge_column = lane + column * (2048 - 128)

    for v in range(SUBSET):

        def one_x(x, total):
            at = (base + v) * XW + x
            fraction = fractions[at]
            pixel = edge_column - (steps[at] - MARGIN)
            weights = (
                jnp.maximum(0.0, 1.0 - fraction) + jnp.maximum(0.0, 0.5 - fraction),
                1.0 - jnp.abs(fraction - 1.0) + (1.0 - jnp.abs(fraction - 0.5)),
                jnp.maximum(0.0, fraction - 0.5),
            )
            for k in range(3):
                inside = (pixel - k >= 0) & (pixel - k < 2048)
                total = total + jnp.where(inside, weights[k], 0.0)
            return total

        edge_sum = lax.fori_loop(0, XW, one_x, zero, unroll=4)
        outer = jnp.maximum(row_total * edge_sum, 1.0)
        slot = rank[base + v]
        take = USED * lax.rem(slot, 2)
        turned = []
        if v % 2 == 0:
            pair_before = before[8 * v : 8 * v + 16, :].astype(F32)
            pair_after = after[8 * v : 8 * v + 16, :].astype(F32)
        low = 8 * (v % 2)
        rows_of[v] = jnp.where(slot >= 2, extra[v][0].astype(F32), images[v][0].astype(F32))
        for j in range(TILES):
            cols = slice(128 * j, 128 * j + 128)
            predicted = (
                own[8 * v : 8 * v + 8, cols]
                + shifted_rows(pair_before[low : low + 8, cols], to_before)
                + shifted_rows(pair_after[low : low + 8, cols], to_after)
            )
            raysum = inner
            if j == 0 or j == TILES - 1:
                raysum = jnp.where(edge_tile == j, outer, inner)
            image = rows_of[v, pl.ds(2 * USED * j + take, 8), :]
            residual = (image - predicted) / raysum
            mixed = back_weights[0] * residual
            for shift in (1, 2):
                mixed = mixed + back_weights[shift] * pltpu.roll(residual, 8 - shift, 0)
            mixed = mixed + pltpu.roll(mixed, 4, 0)
            turned.append(pltpu.roll(mixed, 64, 1))
        frame = [
            jnp.where(lane < 64, a, b) for a, b in zip([zero] + turned, turned + [zero])
        ]
        for shift in range(3):
            if shift == 0:
                rows = frame
            else:
                back = [pltpu.roll(tile, 128 - shift, 1) for tile in frame] + [zero]
                rows = [
                    jnp.where(lane < 128 - shift, back[j], back[j + 1])
                    for j in range(TILES + 1)
                ]
            for j in range(TILES + 1):
                held[v, shift, j] = rows[j]

    def back_x(x, carry):
        here = pl.ds(pl.multiple_of(8 * x, 8), 8)
        totals_x = [zero] * TILES
        for v in range(SUBSET):
            at = (base + v) * XW + x
            step = steps[at]
            coef = taps(fractions[at])
            turned = []
            for j in range(TILES + 1):
                mix = (
                    coef[0] * held[v, 0, j] + coef[1] * held[v, 1, j] + coef[2] * held[v, 2, j]
                )
                turned.append(pltpu.roll(mix, 128 - step, 1))
            mask = lane < 128 - step
            totals_x = [
                totals_x[j] + jnp.where(mask, turned[j], turned[j + 1]) for j in range(TILES)
            ]
        for j in range(TILES):
            moved_state[j, here, :] = state[j, here, :] + (relaxation / SUBSET) * totals_x[j]
        return carry

    lax.fori_loop(0, XW, back_x, 0, unroll=BACK_UNROLL)
    for j in range(TILES):
        for z in range(ZS):
            pair = [moved_state[j, pl.ds(4 * p + z, XW, stride=8), :] for p in range(2)]
            for p in range(2):
                out[z, j, p] = pair[p]
            both = jnp.concatenate(pair, axis=0)
            high = both.astype(jnp.bfloat16)
            out_before[z, j] = high
            out_after[z, j] = high
            if z in (0, ZS - 1):
                rest = (both - high.astype(F32)).astype(jnp.bfloat16)
                (out_before if z == 0 else out_after)[ZS, j] = rest


def update(subset, place, owner, rank, steps, fractions, recv, extra, state, own, before, after):
    base = subset * SUBSET

    def of_view(v):
        return pl.BlockSpec(
            (1, PACKED, 128), lambda i, place, owner, rank, steps, fr: (owner[base + v], 0, 0)
        )

    def whole(array):
        rank_of = array.ndim
        return pl.BlockSpec(array.shape, lambda i, *scalars: (0,) * rank_of)

    spec = pltpu.PrefetchScalarGridSpec(
        num_scalar_prefetch=5,
        grid=(1,),
        in_specs=[of_view(v) for v in range(SUBSET)] * 2
        + [whole(a) for a in (state, own, before, after)],
        out_specs=[whole(a) for a in SLAB_OUT],
        scratch_shapes=[
            pltpu.VMEM((SUBSET, 3, TILES + 1, 8, 128), F32),
            pltpu.VMEM((TILES, 8 * XW, 128), F32),
            pltpu.VMEM((SUBSET, PACKED, 128), F32),
        ],
    )
    return pl.pallas_call(
        functools.partial(update_kernel, base),
        grid_spec=spec,
        out_shape=SLAB_OUT,
        compiler_params=PARAMS,
        name="residual_back",
    )(
        place, owner, rank, steps, fractions,
        *([recv] * SUBSET), *([extra] * SUBSET), state, own, before, after,
    )


def smooth(own, before, after, buffers, along, in_before, in_after, store):
    def first(z, j):
        if ZS <= z < 2 * ZS:
            return [own[z - ZS, j, p] for p in range(2)]
        side = before if z < ZS else after
        both = side[z % ZS, j].astype(F32)
        if z in (ZS - 1, 2 * ZS):
            both = both + side[ZS, j].astype(F32)
        return [both[:XW], both[XW:]]

    row24 = lax.broadcasted_iota(jnp.int32, (XW, 128), 0)
    lane24 = lax.broadcasted_iota(jnp.int32, (XW, 128), 1)
    zero = jnp.zeros((XW, 128), F32)
    for index in range(PASSES):
        low, high = 1 + index, 10 - index
        last = index == PASSES - 1
        target = buffers[index % 2]
        source = buffers[(index + 1) % 2]

        def load(z, j, index=index, source=source):
            if index == 0:
                return first(z, j)
            return [source[z, j, p] for p in range(2)]

        for z in range(low, high + 1):
            along[z] = zero

        def one_tile(j, carry, low=low, high=high, last=last, target=target, load=load):
            following = jnp.minimum(j + 1, TILES - 1)
            has_following = j < TILES - 1
            current = load(low - 1, j)
            flux_before = None
            for z in range(low - 1, high + 1):
                above = load(z + 1, j)
                beside = jnp.where(has_following, load(z, following)[0], 0.0)
                next_even = pltpu.roll(
                    jnp.where(lane24 == 0, beside, current[0]), 127, 1
                )
                ahead = [current[1], next_even]
                fluxes = []
                for p in range(2):
                    c = current[p]
                    dz = above[p] - c
                    dx = jnp.where(row24 < XW - 1, pltpu.roll(c, XW - 1, 0), 0.0) - c
                    dy = ahead[p] - c
                    scale = lax.rsqrt(dz * dz + dx * dx + dy * dy + smooth_floor)
                    fluxes.append((dz * scale, dx * scale, dy * scale))
                flux_z = [fluxes[p][0] for p in range(2)]
                if z < ZS:
                    flux_z = [f * in_before for f in flux_z]
                if z >= low:
                    turned = pltpu.roll(fluxes[1][2], 1, 1)
                    behind_even = jnp.where(lane24 == 0, along[z], turned)
                    along[z] = turned
                    behind = [behind_even, fluxes[0][2]]
                    for p in range(2):
                        flux_x = fluxes[p][1]
                        back_x = jnp.where(row24 > 0, pltpu.roll(flux_x, 1, 0), 0.0)
                        gradient = (
                            (flux_before[p] - fluxes[p][0])
                            + (back_x - flux_x)
                            + (behind[p] - fluxes[p][2])
                        )
                        fresh = current[p] - smooth_step * gradient
                        if z < ZS:
                            fresh = fresh * in_before
                        if z >= 2 * ZS:
                            fresh = fresh * in_after
                        if last:
                            store(z - ZS, j, p, fresh)
                        else:
                            target[z, j, p] = fresh
                flux_before = flux_z
                current = above
            return carry

        lax.fori_loop(0, TILES, one_tile, 0)


SMOOTH_SCRATCH = [
    pltpu.VMEM((3 * ZS, TILES, 2, XW, 128), F32),
    pltpu.VMEM((3 * ZS, TILES, 2, XW, 128), F32),
    pltpu.VMEM((3 * ZS, XW, 128), F32),
]


def smooth_project_kernel(
    place, steps, fractions, own, before, after, state, rows_ref, rows16_ref, one, two, along
):
    def store(z, j, p, value):
        state[j, pl.ds(4 * p + z, XW, stride=8), :] = value

    smooth(
        own, before, after, (one, two), along,
        place[3].astype(F32), place[4].astype(F32), store,
    )
    project(state, steps, fractions, SUBSET, rows_ref, rows16_ref)


def smooth_end_kernel(place, own, before, after, out, one, two, along):
    def store(z, j, p, value):
        two[z, j, p] = value

    smooth(
        own, before, after, (one, two), along,
        place[3].astype(F32), place[4].astype(F32), store,
    )
    matrix = split_matrix(True)
    column = place[0]
    for j in range(TILES - 1):
        pixels = jnp.concatenate(
            [
                jnp.concatenate([two[z, j + column, 0], two[z, j + column, 1]], axis=1)
                for z in range(ZS)
            ],
            axis=0,
        )
        joined = jnp.dot(pixels, matrix, precision=HIGHEST, preferred_element_type=F32)
        out[:, :, 256 * j : 256 * j + 256] = joined.reshape(ZS, XW, 256)


def to_next(value):
    count = lax.axis_size("gz")
    return lax.ppermute(value, "gz", [(i, i + 1) for i in range(count - 1)])


def to_before(value):
    count = lax.axis_size("gz")
    return lax.ppermute(value, "gz", [(i + 1, i) for i in range(count - 1)])


def swap_halves(value):
    return lax.ppermute(value, "col", [(0, 1), (1, 0)])


def fetched(first_slot, *args):
    return lax.all_to_all(pack(first_slot, *args), "gz", 0, 0)


def body(volume, images, owners, subsets, offsets):
    slab_count = lax.axis_size("gz")
    slab = lax.axis_index("gz")
    column = lax.axis_index("col")
    stored = images.shape[0]
    nviews = owners.shape[0]

    edge = swap_halves(jnp.where(column == 0, volume[:, :, -256:], volume[:, :, :256]))
    image_edge = swap_halves(jnp.where(column == 0, images[:, :, -128:], images[:, :, :128]))
    edge, image_edge = lax.optimization_barrier((edge, image_edge))

    views = subsets.reshape(-1)
    recv = fetched(0, owners, views, offsets, images, image_edge)
    positions = jnp.sum(
        jnp.where(
            owners[None, :] == views[:, None], jnp.arange(nviews, dtype=jnp.int32)[None, :], 0
        ),
        axis=1,
    )
    owner = positions // stored
    rank = jnp.sum(
        (
            (owner[None, :] == owner[:, None]) & (positions[None, :] < positions[:, None])
        ).astype(jnp.int32),
        axis=1,
    )
    steps, fractions = view_geometry(views, XW, MARGIN, nviews)
    steps, fractions = steps.reshape(-1), fractions.reshape(-1)

    own_start = offsets[slab]
    before_start = offsets[jnp.maximum(slab - 1, 0)]
    next_start = offsets[jnp.minimum(slab + 1, slab_count - 1)]
    place = jnp.stack(
        [
            column,
            own_start - before_start,
            own_start - next_start,
            (slab > 0).astype(jnp.int32),
            (slab < slab_count - 1).astype(jnp.int32),
        ]
    ).astype(jnp.int32)

    state, rows, rows16 = scalar_call(
        start_kernel, (place, steps, fractions), (volume, edge), ROWS_OUT, [], "split_project"
    )
    later_edge, recv = lax.optimization_barrier((image_edge, recv))
    extra = lax.cond(
        jnp.max(rank) >= 2,
        lambda: fetched(2, owners, views, offsets, images, later_edge),
        lambda: jnp.zeros(recv.shape, recv.dtype),
    )
    for subset in range(SUBSETS):
        fresh, low_side, high_side = update(
            subset, place, owner, rank, steps, fractions, recv, extra,
            state, rows, to_next(rows16), to_before(rows16),
        )
        around = (fresh, to_next(high_side), to_before(low_side))
        if subset < SUBSETS - 1:
            state, rows, rows16 = scalar_call(
                smooth_project_kernel, (place, steps, fractions), around, ROWS_OUT,
                SMOOTH_SCRATCH, "smooth_project",
            )
    return scalar_call(
        smooth_end_kernel, (place,), around,
        jax.ShapeDtypeStruct(volume.shape, F32), SMOOTH_SCRATCH, "smooth_join",
    )


def solution(mesh):
    in_specs = (P("gz", None, "col"), P("gz", None, "col"), P(), P(), P())
    out_specs = P("gz", None, "col")
    return jax.shard_map(body, mesh=mesh, in_specs=in_specs, out_specs=out_specs, check_vma=False)
```

```python
import functools

import jax
import jax.numpy as jnp
from jax import lax
from jax.experimental import pallas as pl
from jax.experimental.pallas import tpu as pltpu
from jax.sharding import PartitionSpec as P

SUBSET = 6
SUBSETS = 2
PASSES = 4
MARGIN = 64

relaxation = 0.8
smooth_step = 0.05
smooth_floor = 0.1

ZS = 4
XW = 24
TILES = 9
WIDE = TILES * 128
USED = 6
OWN = TILES - 1
PACKED = 2 * USED * OWN
CHUNKS = 4
HIGHEST = lax.Precision.HIGHEST
PARAMS = pltpu.CompilerParams(vmem_limit_bytes=48 * 1024 * 1024)
F32 = jnp.float32
PROJECT_UNROLL = 24
BACK_UNROLL = 8


def view_geometry(view, xcount, margin, nviews):
    angles = jnp.pi * view.astype(jnp.float32) / nviews
    across = (2.0 * jnp.arange(xcount, dtype=jnp.float32) - (xcount - 1)) / xcount
    shifted = margin * (
        0.375 * jnp.cos(angles)[:, None] + 0.25 * jnp.sin(angles)[:, None] * across[None, :]
    ) + margin
    integral = jnp.floor(shifted)
    return (integral.astype(jnp.int32), shifted - integral)


def iota2(dim, rows=8):
    return lax.broadcasted_iota(jnp.int32, (rows, 128), dim)


def taps(fraction):
    reach = jnp.where(iota2(0) >= ZS, 0.5, 0.0) + fraction
    return (
        jnp.maximum(0.0, 1.0 - reach),
        1.0 - jnp.abs(reach - 1.0),
        jnp.maximum(0.0, reach - 1.0),
    )


def row_weights(shift, transposed):
    i = iota2(0)
    z = i if transposed else i - shift
    centers = 1.5 * z.astype(F32) + 0.25
    rows = (z + shift).astype(F32)
    weight = jnp.maximum(0.0, 1.0 - jnp.abs(centers - rows))
    return jnp.where((z >= 0) & (z < ZS), weight, 0.0)


def split_matrix(joined):
    r = lax.broadcasted_iota(jnp.int32, (256, 256), 0)
    c = lax.broadcasted_iota(jnp.int32, (256, 256), 1)
    if joined:
        r, c = c, r
    return (r == jnp.where(c < 128, 2 * c, 2 * (c - 128) + 1)).astype(F32)


def project(state, steps, fractions, base, rows_ref, rows16_ref):
    lane = iota2(1)
    weights = [row_weights(shift, False) for shift in range(3)]
    zero = jnp.zeros((8, 128), F32)
    pair = []
    for v in range(SUBSET):

        def one_x(x, sums):
            at = (base + v) * XW + x
            step = steps[at]
            coef = taps(fractions[at])
            here = pl.ds(pl.multiple_of(8 * x, 8), 8)
            turned = [pltpu.roll(state[j, here, :], step, 1) for j in range(TILES)]
            mask = lane >= step
            before = [zero] + turned
            after = turned + [zero]
            moved = [jnp.where(mask, after[j], before[j]) for j in range(TILES + 1)]
            return tuple(
                sums[k * (TILES + 1) + j] + coef[k] * moved[j]
                for k in range(3)
                for j in range(TILES + 1)
            )

        sums = lax.fori_loop(0, XW, one_x, (zero,) * (3 * (TILES + 1)), unroll=PROJECT_UNROLL)
        frame = []
        once = [zero] + [pltpu.roll(sums[TILES + 1 + j], 1, 1) for j in range(TILES + 1)]
        twice = [zero] + [pltpu.roll(sums[2 * TILES + 2 + j], 2, 1) for j in range(TILES + 1)]
        for j in range(TILES + 1):
            total = (
                sums[j]
                + jnp.where(lane >= 1, once[j + 1], once[j])
                + jnp.where(lane >= 2, twice[j + 1], twice[j])
            )
            total = total + pltpu.roll(total, 4, 0)
            rows = (
                weights[0] * total
                + weights[1] * pltpu.roll(total, 1, 0)
                + weights[2] * pltpu.roll(total, 2, 0)
            )
            frame.append(pltpu.roll(rows, 64, 1))
        out = [jnp.where(lane < 64, frame[j], frame[j + 1]) for j in range(TILES)]
        for j in range(TILES):
            rows_ref[8 * v : 8 * v + 8, 128 * j : 128 * j + 128] = out[j]
        pair.append(out)
        if v % 2:
            for j in range(TILES):
                both = jnp.concatenate([pair[v - 1][j], pair[v][j]], axis=0)
                rows16_ref[8 * v - 8 : 8 * v + 8, 128 * j : 128 * j + 128] = both.astype(
                    jnp.bfloat16
                )


def pack_kernel(first_slot, owners, subsets, offsets, images, out, got, held, ready, sems, out_sems):
    slab = lax.axis_index("gz")
    stored = images.shape[0]
    slab_count = out.shape[0]
    count = subsets.shape[0]
    found = jnp.int32(0)
    slots = [jnp.int32(0), jnp.int32(0)]
    for i in range(stored):
        view = owners[stored * slab + i]
        hits = jnp.int32(0)
        for k in range(count):
            hits = hits + (subsets[k] == view).astype(jnp.int32)
        for slot in range(2):
            slots[slot] = jnp.where((hits > 0) & (found == first_slot + slot), i, slots[slot])
        found = found + hits
    copies = [
        pltpu.make_async_copy(images.at[slots[slot]], got.at[slot], sems.at[slot])
        for slot in range(2)
    ]
    for copy in copies:
        copy.start()
    for slot, copy in enumerate(copies):
        copy.wait()
        for j in range(OWN):
            held[slot, j] = got[slot, :, 128 * j : 128 * j + 128].astype(F32)

    row = iota2(0)

    def one_slab(i, carry):
        window = pl.ds(offsets[i], 8)
        parts = []
        for j in range(OWN):
            b = pltpu.roll(held[1, j, window, :], 6, 0)
            a = jnp.where(row < USED, held[0, j, window, :], b)
            if j % 2 == 0:
                parts += [a, b]
            else:
                middle = pltpu.roll(a, 4, 0)
                parts[-1] = jnp.where(row < 4, parts[-1], middle)
                parts.append(jnp.where(row < 4, middle, pltpu.roll(b, 4, 0)))
        ready[i] = jnp.concatenate(parts, axis=0).astype(jnp.bfloat16)
        return carry

    chunk = slab_count // CHUNKS
    sent = []
    for part in range(CHUNKS):
        lax.fori_loop(part * chunk, part * chunk + chunk, one_slab, 0, unroll=2)
        here = pl.ds(part * chunk, chunk)
        sent.append(pltpu.make_async_copy(ready.at[here], out.at[here], out_sems.at[part]))
        sent[-1].start()
    for copy in sent:
        copy.wait()


def pack(first_slot, owners, subsets, offsets, images):
    rows = images.shape[1]
    smem = pl.BlockSpec(memory_space=pltpu.SMEM)
    hbm = pl.BlockSpec(memory_space=pl.ANY)
    shape = (offsets.shape[0], PACKED, 128)
    return pl.pallas_call(
        functools.partial(pack_kernel, first_slot),
        in_specs=[smem] * 3 + [hbm],
        out_specs=hbm,
        out_shape=jax.ShapeDtypeStruct(shape, jnp.bfloat16),
        scratch_shapes=[
            pltpu.VMEM((2, rows, 128 * OWN), jnp.bfloat16),
            pltpu.VMEM((2, OWN, rows, 128), F32),
            pltpu.VMEM(shape, jnp.bfloat16),
            pltpu.SemaphoreType.DMA((2,)),
            pltpu.SemaphoreType.DMA((CHUNKS,)),
        ],
        compiler_params=PARAMS,
        name="pack_images",
    )(owners, subsets, offsets, images)


def edge_kernel(place, owner, rank, *refs):
    count = len(refs) // 2
    out = refs[-1]
    for v in range(count):
        out[v] = jnp.where(rank[v] >= 2, refs[count + v][0].astype(F32), refs[v][0].astype(F32)).astype(
            jnp.bfloat16
        )


def inner_edges(place, owner, rank, recv, extra):
    count = owner.shape[0]
    last = PACKED // 16 - 1

    def of_view(v, direct):
        def index(i, place, owner, rank):
            return (v if direct else owner[v], last * (1 - place[0]), 0)

        return pl.BlockSpec((1, 16, 128), index)

    spec = pltpu.PrefetchScalarGridSpec(
        num_scalar_prefetch=3,
        grid=(1,),
        in_specs=[of_view(v, False) for v in range(count)] + [of_view(v, True) for v in range(count)],
        out_specs=pl.BlockSpec((count, 16, 128), lambda i, *scalars: (0, 0, 0)),
    )
    return pl.pallas_call(
        edge_kernel,
        grid_spec=spec,
        out_shape=jax.ShapeDtypeStruct((count, 16, 128), jnp.bfloat16),
        compiler_params=PARAMS,
        name="inner_edges",
    )(place, owner, rank, *([recv] * count), *([extra] * count))


def start_kernel(place, steps, fractions, volume, edge, state, rows_ref, rows16_ref):
    column = place[0]
    matrix = split_matrix(False)

    def put(pixels, tile):
        halves = jnp.dot(
            pixels.reshape(ZS * XW, 256), matrix, precision=HIGHEST, preferred_element_type=F32
        )
        for z in range(ZS):
            for p in range(2):
                state[tile, pl.ds(4 * p + z, XW, stride=8), :] = halves[
                    XW * z : XW * z + XW, 128 * p : 128 * p + 128
                ]

    for j in range(TILES - 1):
        put(volume[:, :, 256 * j : 256 * j + 256], j + column)
    put(edge[...], (TILES - 1) * (1 - column))
    project(state, steps, fractions, 0, rows_ref, rows16_ref)


def scalar_call(kernel, scalars, arrays, out_shape, scratch, name):
    vmem = pl.BlockSpec(memory_space=pltpu.VMEM)
    smem = pl.BlockSpec(memory_space=pltpu.SMEM)
    single = not isinstance(out_shape, (list, tuple))
    return pl.pallas_call(
        kernel,
        in_specs=[smem] * len(scalars) + [vmem] * len(arrays),
        out_specs=vmem if single else [vmem] * len(out_shape),
        out_shape=out_shape,
        scratch_shapes=scratch,
        compiler_params=PARAMS,
        name=name,
    )(*scalars, *arrays)


ROWS_OUT = (
    jax.ShapeDtypeStruct((TILES, 8 * XW, 128), F32),
    jax.ShapeDtypeStruct((8 * SUBSET, WIDE), F32),
    jax.ShapeDtypeStruct((8 * SUBSET, WIDE), jnp.bfloat16),
)
HALO = jax.ShapeDtypeStruct((ZS + 1, TILES, 2 * XW, 128), jnp.bfloat16)
SLAB_OUT = (jax.ShapeDtypeStruct((ZS, TILES, 2, XW, 128), F32), HALO, HALO)


def update_kernel(base, place, owner, rank, steps, fractions, *refs):
    images, extra = refs[:SUBSET], refs[SUBSET : 2 * SUBSET]
    state, own, before, after, edges, out, out_before, out_after = refs[2 * SUBSET :][:8]
    held, moved_state, packed, packed_edge, rows_of = refs[2 * SUBSET :][8:]
    column, to_before, to_after = place[0], place[1], place[2]
    has_before, has_after = place[3], place[4]
    lane, sub = iota2(1), iota2(0)
    zero = jnp.zeros((8, 128), F32)
    totals = row_weights(0, False) + row_weights(1, False) + row_weights(2, False)

    def shifted_rows(value, by):
        row = sub + by
        turned = pltpu.roll(value, lax.rem(16 - by, 8), 0)
        return jnp.where((row >= 0) & (row < 8), turned, 0.0)

    row_total = (
        totals
        + shifted_rows(totals, to_before) * has_before.astype(F32)
        + shifted_rows(totals, to_after) * has_after.astype(F32)
    )
    inner = jnp.maximum(row_total * float(2 * XW), 1.0)
    back_weights = [row_weights(shift, True) for shift in range(3)]
    edge_tile = column * (TILES - 1)
    edge_column = lane + column * (2048 - 128)

    for v in range(SUBSET):

        def one_x(x, total):
            at = (base + v) * XW + x
            fraction = fractions[at]
            pixel = edge_column - (steps[at] - MARGIN)
            weights = (
                jnp.maximum(0.0, 1.0 - fraction) + jnp.maximum(0.0, 0.5 - fraction),
                1.0 - jnp.abs(fraction - 1.0) + (1.0 - jnp.abs(fraction - 0.5)),
                jnp.maximum(0.0, fraction - 0.5),
            )
            for k in range(3):
                inside = (pixel - k >= 0) & (pixel - k < 2048)
                total = total + jnp.where(inside, weights[k], 0.0)
            return total

        edge_sum = lax.fori_loop(0, XW, one_x, zero, unroll=4)
        outer = jnp.maximum(row_total * edge_sum, 1.0)
        slot = rank[base + v]
        take = USED * lax.rem(slot, 2)
        turned = []
        if v % 2 == 0:
            pair_before = before[8 * v : 8 * v + 16, :].astype(F32)
            pair_after = after[8 * v : 8 * v + 16, :].astype(F32)
        low = 8 * (v % 2)
        packed[v, :PACKED] = jnp.where(
            slot >= 2, extra[v][0].astype(F32), images[v][0].astype(F32)
        )
        packed_edge[v, :16] = edges[base + v].astype(F32)
        for j in range(OWN):
            rows_of[v, j + column] = packed[v, pl.ds(2 * USED * j + take, 8), :]
        rows_of[v, OWN * (1 - column)] = packed_edge[v, pl.ds(4 * column + take, 8), :]
        for j in range(TILES):
            cols = slice(128 * j, 128 * j + 128)
            predicted = (
                own[8 * v : 8 * v + 8, cols]
                + shifted_rows(pair_before[low : low + 8, cols], to_before)
                + shifted_rows(pair_after[low : low + 8, cols], to_after)
            )
            raysum = inner
            if j == 0 or j == TILES - 1:
                raysum = jnp.where(edge_tile == j, outer, inner)
            residual = jnp.where(sub < USED, (rows_of[v, j] - predicted) / raysum, 0.0)
            mixed = back_weights[0] * residual
            for shift in (1, 2):
                mixed = mixed + back_weights[shift] * pltpu.roll(residual, 8 - shift, 0)
            mixed = mixed + pltpu.roll(mixed, 4, 0)
            turned.append(pltpu.roll(mixed, 64, 1))
        frame = [
            jnp.where(lane < 64, a, b) for a, b in zip([zero] + turned, turned + [zero])
        ]
        for shift in range(3):
            if shift == 0:
                rows = frame
            else:
                back = [pltpu.roll(tile, 128 - shift, 1) for tile in frame] + [zero]
                rows = [
                    jnp.where(lane < 128 - shift, back[j], back[j + 1])
                    for j in range(TILES + 1)
                ]
            for j in range(TILES + 1):
                held[v, shift, j] = rows[j]

    def back_x(x, carry):
        here = pl.ds(pl.multiple_of(8 * x, 8), 8)
        totals_x = [zero] * TILES
        for v in range(SUBSET):
            at = (base + v) * XW + x
            step = steps[at]
            coef = taps(fractions[at])
            turned = []
            for j in range(TILES + 1):
                mix = (
                    coef[0] * held[v, 0, j] + coef[1] * held[v, 1, j] + coef[2] * held[v, 2, j]
                )
                turned.append(pltpu.roll(mix, 128 - step, 1))
            mask = lane < 128 - step
            totals_x = [
                totals_x[j] + jnp.where(mask, turned[j], turned[j + 1]) for j in range(TILES)
            ]
        for j in range(TILES):
            moved_state[j, here, :] = state[j, here, :] + (relaxation / SUBSET) * totals_x[j]
        return carry

    lax.fori_loop(0, XW, back_x, 0, unroll=BACK_UNROLL)
    for j in range(TILES):
        for z in range(ZS):
            pair = [moved_state[j, pl.ds(4 * p + z, XW, stride=8), :] for p in range(2)]
            for p in range(2):
                out[z, j, p] = pair[p]
            both = jnp.concatenate(pair, axis=0)
            high = both.astype(jnp.bfloat16)
            out_before[z, j] = high
            out_after[z, j] = high
            if z in (0, ZS - 1):
                rest = (both - high.astype(F32)).astype(jnp.bfloat16)
                (out_before if z == 0 else out_after)[ZS, j] = rest


def update(subset, place, owner, rank, steps, fractions, recv, extra, state, own, before, after, edges):
    base = subset * SUBSET

    def of_view(v, direct):
        def index(i, place, owner, rank, steps, fractions):
            return (base + v if direct else owner[base + v], 0, 0)

        return pl.BlockSpec((1, PACKED, 128), index)

    def whole(array):
        rank_of = array.ndim
        return pl.BlockSpec(array.shape, lambda i, *scalars: (0,) * rank_of)

    spec = pltpu.PrefetchScalarGridSpec(
        num_scalar_prefetch=5,
        grid=(1,),
        in_specs=[of_view(v, False) for v in range(SUBSET)]
        + [of_view(v, True) for v in range(SUBSET)]
        + [whole(a) for a in (state, own, before, after, edges)],
        out_specs=[whole(a) for a in SLAB_OUT],
        scratch_shapes=[
            pltpu.VMEM((SUBSET, 3, TILES + 1, 8, 128), F32),
            pltpu.VMEM((TILES, 8 * XW, 128), F32),
            pltpu.VMEM((SUBSET, PACKED + 8, 128), F32),
            pltpu.VMEM((SUBSET, 24, 128), F32),
            pltpu.VMEM((SUBSET, TILES, 8, 128), F32),
        ],
    )
    return pl.pallas_call(
        functools.partial(update_kernel, base),
        grid_spec=spec,
        out_shape=SLAB_OUT,
        compiler_params=PARAMS,
        name="residual_back",
    )(
        place, owner, rank, steps, fractions,
        *([recv] * SUBSET), *([extra] * SUBSET), state, own, before, after, edges,
    )


def smooth(own, before, after, buffers, along, in_before, in_after, store):
    def first(z, j):
        if ZS <= z < 2 * ZS:
            return [own[z - ZS, j, p] for p in range(2)]
        side = before if z < ZS else after
        both = side[z % ZS, j].astype(F32)
        if z in (ZS - 1, 2 * ZS):
            both = both + side[ZS, j].astype(F32)
        return [both[:XW], both[XW:]]

    row24 = lax.broadcasted_iota(jnp.int32, (XW, 128), 0)
    lane24 = lax.broadcasted_iota(jnp.int32, (XW, 128), 1)
    zero = jnp.zeros((XW, 128), F32)
    for index in range(PASSES):
        low, high = 1 + index, 10 - index
        last = index == PASSES - 1
        target = buffers[index % 2]
        source = buffers[(index + 1) % 2]

        def load(z, j, index=index, source=source):
            if index == 0:
                return first(z, j)
            return [source[z, j, p] for p in range(2)]

        for z in range(low, high + 1):
            along[z] = zero

        def one_tile(j, carry, low=low, high=high, last=last, target=target, load=load):
            following = jnp.minimum(j + 1, TILES - 1)
            has_following = j < TILES - 1
            current = load(low - 1, j)
            flux_before = None
            for z in range(low - 1, high + 1):
                above = load(z + 1, j)
                beside = jnp.where(has_following, load(z, following)[0], 0.0)
                next_even = pltpu.roll(
                    jnp.where(lane24 == 0, beside, current[0]), 127, 1
                )
                ahead = [current[1], next_even]
                fluxes = []
                for p in range(2):
                    c = current[p]
                    dz = above[p] - c
                    dx = jnp.where(row24 < XW - 1, pltpu.roll(c, XW - 1, 0), 0.0) - c
                    dy = ahead[p] - c
                    scale = lax.rsqrt(dz * dz + dx * dx + dy * dy + smooth_floor)
                    fluxes.append((dz * scale, dx * scale, dy * scale))
                flux_z = [fluxes[p][0] for p in range(2)]
                if z < ZS:
                    flux_z = [f * in_before for f in flux_z]
                if z >= low:
                    turned = pltpu.roll(fluxes[1][2], 1, 1)
                    behind_even = jnp.where(lane24 == 0, along[z], turned)
                    along[z] = turned
                    behind = [behind_even, fluxes[0][2]]
                    for p in range(2):
                        flux_x = fluxes[p][1]
                        back_x = jnp.where(row24 > 0, pltpu.roll(flux_x, 1, 0), 0.0)
                        gradient = (
                            (flux_before[p] - fluxes[p][0])
                            + (back_x - flux_x)
                            + (behind[p] - fluxes[p][2])
                        )
                        fresh = current[p] - smooth_step * gradient
                        if z < ZS:
                            fresh = fresh * in_before
                        if z >= 2 * ZS:
                            fresh = fresh * in_after
                        if last:
                            store(z - ZS, j, p, fresh)
                        else:
                            target[z, j, p] = fresh
                flux_before = flux_z
                current = above
            return carry

        lax.fori_loop(0, TILES, one_tile, 0)


SMOOTH_SCRATCH = [
    pltpu.VMEM((3 * ZS, TILES, 2, XW, 128), F32),
    pltpu.VMEM((3 * ZS, TILES, 2, XW, 128), F32),
    pltpu.VMEM((3 * ZS, XW, 128), F32),
]


def smooth_project_kernel(
    place, steps, fractions, own, before, after, state, rows_ref, rows16_ref, one, two, along
):
    def store(z, j, p, value):
        state[j, pl.ds(4 * p + z, XW, stride=8), :] = value

    smooth(
        own, before, after, (one, two), along,
        place[3].astype(F32), place[4].astype(F32), store,
    )
    project(state, steps, fractions, SUBSET, rows_ref, rows16_ref)


def smooth_end_kernel(place, own, before, after, out, one, two, along):
    def store(z, j, p, value):
        two[z, j, p] = value

    smooth(
        own, before, after, (one, two), along,
        place[3].astype(F32), place[4].astype(F32), store,
    )
    matrix = split_matrix(True)
    column = place[0]
    for j in range(TILES - 1):
        pixels = jnp.concatenate(
            [
                jnp.concatenate([two[z, j + column, 0], two[z, j + column, 1]], axis=1)
                for z in range(ZS)
            ],
            axis=0,
        )
        joined = jnp.dot(pixels, matrix, precision=HIGHEST, preferred_element_type=F32)
        out[:, :, 256 * j : 256 * j + 256] = joined.reshape(ZS, XW, 256)


def to_next(value):
    count = lax.axis_size("gz")
    return lax.ppermute(value, "gz", [(i, i + 1) for i in range(count - 1)])


def to_before(value):
    count = lax.axis_size("gz")
    return lax.ppermute(value, "gz", [(i + 1, i) for i in range(count - 1)])


def swap_halves(value):
    return lax.ppermute(value, "col", [(0, 1), (1, 0)])


def body(volume, images, owners, subsets, offsets):
    slab_count = lax.axis_size("gz")
    slab = lax.axis_index("gz")
    column = lax.axis_index("col")
    stored = images.shape[0]
    nviews = owners.shape[0]

    edge = swap_halves(jnp.where(column == 0, volume[:, :, -256:], volume[:, :, :256]))
    views = subsets.reshape(-1)
    packed = pack(0, owners, views, offsets, images)
    packed, edge = lax.optimization_barrier((packed, edge))
    recv = lax.all_to_all(packed, "gz", 0, 0)

    positions = jnp.sum(
        jnp.where(
            owners[None, :] == views[:, None], jnp.arange(nviews, dtype=jnp.int32)[None, :], 0
        ),
        axis=1,
    )
    owner = positions // stored
    rank = jnp.sum(
        (
            (owner[None, :] == owner[:, None]) & (positions[None, :] < positions[:, None])
        ).astype(jnp.int32),
        axis=1,
    )
    steps, fractions = view_geometry(views, XW, MARGIN, nviews)
    steps, fractions = steps.reshape(-1), fractions.reshape(-1)

    own_start = offsets[slab]
    before_start = offsets[jnp.maximum(slab - 1, 0)]
    next_start = offsets[jnp.minimum(slab + 1, slab_count - 1)]
    place = jnp.stack(
        [
            column,
            own_start - before_start,
            own_start - next_start,
            (slab > 0).astype(jnp.int32),
            (slab < slab_count - 1).astype(jnp.int32),
        ]
    ).astype(jnp.int32)

    state, rows, rows16 = scalar_call(
        start_kernel, (place, steps, fractions), (volume, edge), ROWS_OUT, [], "split_project"
    )
    later_images, recv = lax.optimization_barrier((images, recv))

    def fetch_more():
        more = lax.all_to_all(pack(2, owners, views, offsets, later_images), "gz", 0, 0)
        return more[owner]

    extra = lax.cond(
        jnp.max(rank) >= 2,
        fetch_more,
        lambda: jnp.zeros((views.shape[0],) + recv.shape[1:], recv.dtype),
    )
    edges = swap_halves(inner_edges(place, owner, rank, recv, extra))
    for subset in range(SUBSETS):
        fresh, low_side, high_side = update(
            subset, place, owner, rank, steps, fractions, recv, extra,
            state, rows, to_next(rows16), to_before(rows16), edges,
        )
        around = (fresh, to_next(high_side), to_before(low_side))
        if subset < SUBSETS - 1:
            state, rows, rows16 = scalar_call(
                smooth_project_kernel, (place, steps, fractions), around, ROWS_OUT,
                SMOOTH_SCRATCH, "smooth_project",
            )
    return scalar_call(
        smooth_end_kernel, (place,), around,
        jax.ShapeDtypeStruct(volume.shape, F32), SMOOTH_SCRATCH, "smooth_join",
    )


def solution(mesh):
    in_specs = (P("gz", None, "col"), P("gz", None, "col"), P(), P(), P())
    out_specs = P("gz", None, "col")
    return jax.shard_map(body, mesh=mesh, in_specs=in_specs, out_specs=out_specs, check_vma=False)
```

```python
import functools

import jax
import jax.numpy as jnp
from jax import lax
from jax.experimental import pallas as pl
from jax.experimental.pallas import tpu as pltpu
from jax.sharding import PartitionSpec as P

SUBSET = 6
SUBSETS = 2
PASSES = 4
MARGIN = 64

relaxation = 0.8
smooth_step = 0.05
smooth_floor = 0.1
SCALE = 20.0

ZS = 4
XW = 24
TILES = 9
WIDE = TILES * 128
USED = 6
OWN = TILES - 1
PACKED = 2 * USED * OWN
CHUNKS = 4
HIGHEST = lax.Precision.HIGHEST
PARAMS = pltpu.CompilerParams(vmem_limit_bytes=48 * 1024 * 1024)
F32 = jnp.float32
PROJECT_UNROLL = 24
BACK_UNROLL = 8


def view_geometry(view, xcount, margin, nviews):
    angles = jnp.pi * view.astype(jnp.float32) / nviews
    across = (2.0 * jnp.arange(xcount, dtype=jnp.float32) - (xcount - 1)) / xcount
    shifted = margin * (
        0.375 * jnp.cos(angles)[:, None] + 0.25 * jnp.sin(angles)[:, None] * across[None, :]
    ) + margin
    integral = jnp.floor(shifted)
    return (integral.astype(jnp.int32), shifted - integral)


def iota2(dim, rows=8):
    return lax.broadcasted_iota(jnp.int32, (rows, 128), dim)


def taps(fraction):
    reach = jnp.where(iota2(0) >= ZS, 0.5, 0.0) + fraction
    return (
        jnp.maximum(0.0, 1.0 - reach),
        1.0 - jnp.abs(reach - 1.0),
        jnp.maximum(0.0, reach - 1.0),
    )


def row_weights(shift, transposed):
    i = iota2(0)
    z = i if transposed else i - shift
    centers = 1.5 * z.astype(F32) + 0.25
    rows = (z + shift).astype(F32)
    weight = jnp.maximum(0.0, 1.0 - jnp.abs(centers - rows))
    return jnp.where((z >= 0) & (z < ZS), weight, 0.0)


def split_matrix(joined):
    r = lax.broadcasted_iota(jnp.int32, (256, 256), 0)
    c = lax.broadcasted_iota(jnp.int32, (256, 256), 1)
    if joined:
        r, c = c, r
    return (r == jnp.where(c < 128, 2 * c, 2 * (c - 128) + 1)).astype(F32)


def project(state, steps, fractions, base, rows_ref, rows16_ref):
    lane = iota2(1)
    weights = [row_weights(shift, False) for shift in range(3)]
    zero = jnp.zeros((8, 128), F32)
    pair = []
    for v in range(SUBSET):

        def one_x(x, sums):
            at = (base + v) * XW + x
            step = steps[at]
            coef = taps(fractions[at])
            here = pl.ds(pl.multiple_of(8 * x, 8), 8)
            turned = [pltpu.roll(state[j, here, :], step, 1) for j in range(TILES)]
            mask = lane >= step
            before = [zero] + turned
            after = turned + [zero]
            moved = [jnp.where(mask, after[j], before[j]) for j in range(TILES + 1)]
            return tuple(
                sums[k * (TILES + 1) + j] + coef[k] * moved[j]
                for k in range(3)
                for j in range(TILES + 1)
            )

        sums = lax.fori_loop(0, XW, one_x, (zero,) * (3 * (TILES + 1)), unroll=PROJECT_UNROLL)
        frame = []
        once = [zero] + [pltpu.roll(sums[TILES + 1 + j], 1, 1) for j in range(TILES + 1)]
        twice = [zero] + [pltpu.roll(sums[2 * TILES + 2 + j], 2, 1) for j in range(TILES + 1)]
        for j in range(TILES + 1):
            total = (
                sums[j]
                + jnp.where(lane >= 1, once[j + 1], once[j])
                + jnp.where(lane >= 2, twice[j + 1], twice[j])
            )
            total = total + pltpu.roll(total, 4, 0)
            rows = (
                weights[0] * total
                + weights[1] * pltpu.roll(total, 1, 0)
                + weights[2] * pltpu.roll(total, 2, 0)
            )
            frame.append(pltpu.roll(rows, 64, 1))
        out = [jnp.where(lane < 64, frame[j], frame[j + 1]) for j in range(TILES)]
        for j in range(TILES):
            rows_ref[8 * v : 8 * v + 8, 128 * j : 128 * j + 128] = out[j]
        pair.append(out)
        if v % 2:
            for j in range(TILES):
                both = jnp.concatenate([pair[v - 1][j], pair[v][j]], axis=0)
                rows16_ref[8 * v - 8 : 8 * v + 8, 128 * j : 128 * j + 128] = both.astype(
                    jnp.bfloat16
                )


def pack_kernel(first_slot, owners, subsets, offsets, images, out, got, held, ready, sems, out_sems):
    slab = lax.axis_index("gz")
    stored = images.shape[0]
    slab_count = out.shape[0]
    count = SUBSETS * SUBSET
    found = jnp.int32(0)
    slots = [jnp.int32(0), jnp.int32(0)]
    for i in range(stored):
        view = owners[stored * slab + i]
        hits = jnp.int32(0)
        for k in range(count):
            hits = hits + (subsets[k // SUBSET, k % SUBSET] == view).astype(jnp.int32)
        for slot in range(2):
            slots[slot] = jnp.where((hits > 0) & (found == first_slot + slot), i, slots[slot])
        found = found + hits
    copies = [
        pltpu.make_async_copy(images.at[slots[slot]], got.at[slot], sems.at[slot])
        for slot in range(2)
    ]
    for copy in copies:
        copy.start()
    for slot, copy in enumerate(copies):
        copy.wait()
        for j in range(OWN):
            held[slot, j] = got[slot, :, 128 * j : 128 * j + 128].astype(F32)

    row = iota2(0)

    def one_slab(i, carry):
        window = pl.ds(offsets[i], 8)
        parts = []
        for j in range(OWN):
            b = pltpu.roll(held[1, j, window, :], 6, 0)
            a = jnp.where(row < USED, held[0, j, window, :], b)
            if j % 2 == 0:
                parts += [a, b]
            else:
                middle = pltpu.roll(a, 4, 0)
                parts[-1] = jnp.where(row < 4, parts[-1], middle)
                parts.append(jnp.where(row < 4, middle, pltpu.roll(b, 4, 0)))
        ready[i] = jnp.concatenate(parts, axis=0).astype(jnp.bfloat16)
        return carry

    chunk = slab_count // CHUNKS
    sent = []
    for part in range(CHUNKS):
        lax.fori_loop(part * chunk, part * chunk + chunk, one_slab, 0, unroll=4)
        here = pl.ds(part * chunk, chunk)
        sent.append(pltpu.make_async_copy(ready.at[here], out.at[here], out_sems.at[part]))
        sent[-1].start()
    for copy in sent:
        copy.wait()


def pack(first_slot, owners, subsets, offsets, images):
    rows = images.shape[1]
    smem = pl.BlockSpec(memory_space=pltpu.SMEM)
    hbm = pl.BlockSpec(memory_space=pl.ANY)
    shape = (offsets.shape[0], PACKED, 128)
    return pl.pallas_call(
        functools.partial(pack_kernel, first_slot),
        in_specs=[smem] * 3 + [hbm],
        out_specs=hbm,
        out_shape=jax.ShapeDtypeStruct(shape, jnp.bfloat16),
        scratch_shapes=[
            pltpu.VMEM((2, rows, 128 * OWN), jnp.bfloat16),
            pltpu.VMEM((2, OWN, rows, 128), F32),
            pltpu.VMEM(shape, jnp.bfloat16),
            pltpu.SemaphoreType.DMA((2,)),
            pltpu.SemaphoreType.DMA((CHUNKS,)),
        ],
        compiler_params=PARAMS,
        name="pack_images",
    )(owners, subsets, offsets, images)


def edge_kernel(place, owner, rank, *refs):
    count = len(refs) // 2
    out = refs[-1]
    for v in range(count):
        out[v] = jnp.where(rank[v] >= 2, refs[count + v][0].astype(F32), refs[v][0].astype(F32)).astype(
            jnp.bfloat16
        )


def inner_edges(place, owner, rank, recv, extra):
    count = owner.shape[0]
    last = PACKED // 16 - 1

    def of_view(v, direct):
        def index(i, place, owner, rank):
            return (v if direct else owner[v], last * (1 - place[0]), 0)

        return pl.BlockSpec((1, 16, 128), index)

    spec = pltpu.PrefetchScalarGridSpec(
        num_scalar_prefetch=3,
        grid=(1,),
        in_specs=[of_view(v, False) for v in range(count)] + [of_view(v, True) for v in range(count)],
        out_specs=pl.BlockSpec((count, 16, 128), lambda i, *scalars: (0, 0, 0)),
    )
    return pl.pallas_call(
        edge_kernel,
        grid_spec=spec,
        out_shape=jax.ShapeDtypeStruct((count, 16, 128), jnp.bfloat16),
        compiler_params=PARAMS,
        name="inner_edges",
    )(place, owner, rank, *([recv] * count), *([extra] * count))


def start_kernel(place, steps, fractions, volume, edge, state, rows_ref, rows16_ref):
    column = place[0]
    matrix = split_matrix(False)

    def put(pixels, tile):
        halves = jnp.dot(
            pixels.reshape(ZS * XW, 256), matrix, precision=HIGHEST, preferred_element_type=F32
        )
        for z in range(ZS):
            for p in range(2):
                state[tile, pl.ds(4 * p + z, XW, stride=8), :] = halves[
                    XW * z : XW * z + XW, 128 * p : 128 * p + 128
                ]

    for j in range(TILES - 1):
        put(volume[:, :, 256 * j : 256 * j + 256], j + column)
    put(edge[...], (TILES - 1) * (1 - column))
    project(state, steps, fractions, 0, rows_ref, rows16_ref)


def scalar_call(kernel, scalars, arrays, out_shape, scratch, name):
    vmem = pl.BlockSpec(memory_space=pltpu.VMEM)
    smem = pl.BlockSpec(memory_space=pltpu.SMEM)
    single = not isinstance(out_shape, (list, tuple))
    return pl.pallas_call(
        kernel,
        in_specs=[smem] * len(scalars) + [vmem] * len(arrays),
        out_specs=vmem if single else [vmem] * len(out_shape),
        out_shape=out_shape,
        scratch_shapes=scratch,
        compiler_params=PARAMS,
        name=name,
    )(*scalars, *arrays)


ROWS_OUT = (
    jax.ShapeDtypeStruct((TILES, 8 * XW, 128), F32),
    jax.ShapeDtypeStruct((8 * SUBSET, WIDE), F32),
    jax.ShapeDtypeStruct((8 * SUBSET, WIDE), jnp.bfloat16),
)
HALO = jax.ShapeDtypeStruct((ZS + 1, TILES, 2 * XW, 128), jnp.bfloat16)
SLAB_OUT = (jax.ShapeDtypeStruct((ZS, TILES, 2, XW, 128), F32), HALO, HALO)


def update_kernel(base, place, owner, rank, steps, fractions, *refs):
    images, extra = refs[:SUBSET], refs[SUBSET : 2 * SUBSET]
    state, own, before, after, edges, out, out_before, out_after = refs[2 * SUBSET :][:8]
    held, moved_state, packed, packed_edge, rows_of = refs[2 * SUBSET :][8:]
    column, to_before, to_after = place[0], place[1], place[2]
    has_before, has_after = place[3], place[4]
    lane, sub = iota2(1), iota2(0)
    zero = jnp.zeros((8, 128), F32)
    totals = row_weights(0, False) + row_weights(1, False) + row_weights(2, False)

    def shifted_rows(value, by):
        row = sub + by
        turned = pltpu.roll(value, lax.rem(16 - by, 8), 0)
        return jnp.where((row >= 0) & (row < 8), turned, 0.0)

    row_total = (
        totals
        + shifted_rows(totals, to_before) * has_before.astype(F32)
        + shifted_rows(totals, to_after) * has_after.astype(F32)
    )
    inner = jnp.maximum(row_total * float(2 * XW), 1.0)
    back_weights = [row_weights(shift, True) for shift in range(3)]
    edge_tile = column * (TILES - 1)
    edge_column = lane + column * (2048 - 128)

    for v in range(SUBSET):

        def one_x(x, total):
            at = (base + v) * XW + x
            fraction = fractions[at]
            pixel = edge_column - (steps[at] - MARGIN)
            weights = (
                jnp.maximum(0.0, 1.0 - fraction) + jnp.maximum(0.0, 0.5 - fraction),
                1.0 - jnp.abs(fraction - 1.0) + (1.0 - jnp.abs(fraction - 0.5)),
                jnp.maximum(0.0, fraction - 0.5),
            )
            for k in range(3):
                inside = (pixel - k >= 0) & (pixel - k < 2048)
                total = total + jnp.where(inside, weights[k], 0.0)
            return total

        edge_sum = lax.fori_loop(0, XW, one_x, zero, unroll=4)
        outer = jnp.maximum(row_total * edge_sum, 1.0)
        slot = rank[base + v]
        take = USED * lax.rem(slot, 2)
        turned = []
        if v % 2 == 0:
            pair_before = before[8 * v : 8 * v + 16, :].astype(F32)
            pair_after = after[8 * v : 8 * v + 16, :].astype(F32)
        low = 8 * (v % 2)
        packed[v, :PACKED] = jnp.where(
            slot >= 2, extra[v][0].astype(F32), images[v][0].astype(F32)
        )
        packed_edge[v, :16] = edges[base + v].astype(F32)
        for j in range(OWN):
            rows_of[v, j + column] = packed[v, pl.ds(2 * USED * j + take, 8), :]
        rows_of[v, OWN * (1 - column)] = packed_edge[v, pl.ds(4 * column + take, 8), :]
        for j in range(TILES):
            cols = slice(128 * j, 128 * j + 128)
            predicted = (
                own[8 * v : 8 * v + 8, cols]
                + shifted_rows(pair_before[low : low + 8, cols], to_before)
                + shifted_rows(pair_after[low : low + 8, cols], to_after)
            )
            raysum = inner
            if j == 0 or j == TILES - 1:
                raysum = jnp.where(edge_tile == j, outer, inner)
            residual = jnp.where(sub < USED, (rows_of[v, j] - predicted) / raysum, 0.0)
            mixed = back_weights[0] * residual
            for shift in (1, 2):
                mixed = mixed + back_weights[shift] * pltpu.roll(residual, 8 - shift, 0)
            mixed = mixed + pltpu.roll(mixed, 4, 0)
            turned.append(pltpu.roll(mixed, 64, 1))
        frame = [
            jnp.where(lane < 64, a, b) for a, b in zip([zero] + turned, turned + [zero])
        ]
        moved = [frame]
        for shift in (1, 2):
            back = [pltpu.roll(tile, 128 - shift, 1) for tile in frame] + [zero]
            moved.append(
                [
                    jnp.where(lane < 128 - shift, back[j], back[j + 1])
                    for j in range(TILES + 1)
                ]
            )
        for j in range(TILES + 1):
            held[v, 0, j] = moved[0][j]
            held[v, 1, j] = moved[1][j]
            held[v, 2, j] = jnp.where(sub < ZS, moved[0][j], moved[1][j])
            held[v, 3, j] = jnp.where(sub < ZS, moved[1][j], moved[2][j])

    def back_x(x, carry):
        here = pl.ds(pl.multiple_of(8 * x, 8), 8)
        totals_x = [zero] * TILES
        for v in range(SUBSET):
            at = (base + v) * XW + x
            step = steps[at]
            fraction = fractions[at]
            late = (fraction >= 0.5).astype(jnp.int32)
            near = 1.0 - fraction + jnp.where(sub >= ZS, late.astype(F32) - 0.5, 0.0)
            far = 1.0 - near
            turned = []
            for j in range(TILES + 1):
                mix = near * held[v, 2 * late, j] + far * held[v, 2 * late + 1, j]
                turned.append(pltpu.roll(mix, 128 - step, 1))
            mask = lane < 128 - step
            totals_x = [
                totals_x[j] + jnp.where(mask, turned[j], turned[j + 1]) for j in range(TILES)
            ]
        for j in range(TILES):
            moved_state[j, here, :] = (
                SCALE * state[j, here, :] + (SCALE * relaxation / SUBSET) * totals_x[j]
            )
        return carry

    lax.fori_loop(0, XW, back_x, 0, unroll=BACK_UNROLL)
    for j in range(TILES):
        for z in range(ZS):
            pair = [moved_state[j, pl.ds(4 * p + z, XW, stride=8), :] for p in range(2)]
            for p in range(2):
                out[z, j, p] = pair[p]
            both = jnp.concatenate(pair, axis=0)
            high = both.astype(jnp.bfloat16)
            out_before[z, j] = high
            out_after[z, j] = high
            if z in (0, ZS - 1):
                rest = (both - high.astype(F32)).astype(jnp.bfloat16)
                (out_before if z == 0 else out_after)[ZS, j] = rest


def update(subset, place, owner, rank, steps, fractions, recv, extra, state, own, before, after, edges):
    base = subset * SUBSET

    def of_view(v, direct):
        def index(i, place, owner, rank, steps, fractions):
            return (base + v if direct else owner[base + v], 0, 0)

        return pl.BlockSpec((1, PACKED, 128), index)

    def whole(array):
        rank_of = array.ndim
        return pl.BlockSpec(array.shape, lambda i, *scalars: (0,) * rank_of)

    spec = pltpu.PrefetchScalarGridSpec(
        num_scalar_prefetch=5,
        grid=(1,),
        in_specs=[of_view(v, False) for v in range(SUBSET)]
        + [of_view(v, True) for v in range(SUBSET)]
        + [whole(a) for a in (state, own, before, after, edges)],
        out_specs=[whole(a) for a in SLAB_OUT],
        scratch_shapes=[
            pltpu.VMEM((SUBSET, 4, TILES + 1, 8, 128), F32),
            pltpu.VMEM((TILES, 8 * XW, 128), F32),
            pltpu.VMEM((SUBSET, PACKED + 8, 128), F32),
            pltpu.VMEM((SUBSET, 24, 128), F32),
            pltpu.VMEM((SUBSET, TILES, 8, 128), F32),
        ],
    )
    return pl.pallas_call(
        functools.partial(update_kernel, base),
        grid_spec=spec,
        out_shape=SLAB_OUT,
        compiler_params=PARAMS,
        name="residual_back",
    )(
        place, owner, rank, steps, fractions,
        *([recv] * SUBSET), *([extra] * SUBSET), state, own, before, after, edges,
    )


def smooth(own, before, after, buffers, along, in_before, in_after, store):
    sub, lane = iota2(0), iota2(1)
    zero = jnp.zeros((8, 128), F32)
    blocks = range(XW // 8)
    first_lane, not_last, not_first = lane == 0, sub < 7, sub > 0

    def first(z, j):
        if ZS <= z < 2 * ZS:
            both = [own[z - ZS, j, p] for p in range(2)]
        else:
            side = before if z < ZS else after
            joined = side[z % ZS, j].astype(F32)
            if z in (ZS - 1, 2 * ZS):
                joined = joined + side[ZS, j].astype(F32)
            both = [joined[:XW], joined[XW:]]
        return [[both[p][8 * i : 8 * i + 8] for i in blocks] for p in range(2)]

    for index in range(PASSES):
        low, high = 1 + index, 10 - index
        last = index == PASSES - 1
        target = buffers[index % 2]
        source = buffers[(index + 1) % 2]

        def load(z, j, index=index, source=source):
            if index == 0:
                return first(z, j)
            return [[source[z, j, p, 8 * i : 8 * i + 8] for i in blocks] for p in range(2)]

        def next_row(z, j, p, values, index=index, source=source):
            if index == 0:
                turned = [pltpu.roll(value, 7, 0) for value in values] + [zero]
                return [jnp.where(not_last, turned[i], turned[i + 1]) for i in blocks]
            moved = [source[z, j, p, 8 * i + 1 : 8 * i + 9] for i in blocks]
            moved[-1] = jnp.where(not_last, moved[-1], 0.0)
            return moved

        for z in range(low, high + 1):
            along[z] = jnp.zeros((XW, 128), F32)

        def one_tile(
            j, carry, low=low, high=high, last=last, target=target, load=load, next_row=next_row
        ):
            following = jnp.minimum(j + 1, TILES - 1)
            has_following = (j < TILES - 1).astype(F32)
            current = load(low - 1, j)
            flux_before = None
            for z in range(low - 1, high + 1):
                above = load(z + 1, j)
                beside = load(z, following)[0]
                next_even = [
                    pltpu.roll(
                        jnp.where(first_lane, beside[i] * has_following, current[0][i]), 127, 1
                    )
                    for i in blocks
                ]
                ahead = [current[1], next_even]
                flux_z, flux_x, flux_y = [], [], []
                for p in range(2):
                    c = current[p]
                    row_next = next_row(z, j, p, c)
                    for i in blocks:
                        dz = above[p][i] - c[i]
                        dx = row_next[i] - c[i]
                        dy = ahead[p][i] - c[i]
                        scale = lax.rsqrt(
                            dz * dz + dx * dx + dy * dy + smooth_floor * SCALE * SCALE
                        )
                        flux_z.append(dz * scale)
                        flux_x.append(dx * scale)
                        flux_y.append(dy * scale)
                count = len(blocks)
                if z >= low:
                    turned = [pltpu.roll(flux_y[count + i], 1, 1) for i in blocks]
                    behind = [
                        jnp.where(first_lane, along[z, 8 * i : 8 * i + 8], turned[i])
                        for i in blocks
                    ] + flux_y[:count]
                    for i in blocks:
                        along[z, 8 * i : 8 * i + 8] = turned[i]
                    for p in range(2):
                        rolled = [
                            pltpu.roll(flux_x[count * p + i], 1, 0) for i in blocks
                        ]
                        rolled = [zero] + rolled
                        for i in blocks:
                            k = count * p + i
                            row_before = jnp.where(not_first, rolled[i + 1], rolled[i])
                            fresh = (
                                current[p][i]
                                + (flux_z[k] - flux_before[k])
                                + (flux_x[k] - row_before)
                                + (flux_y[k] - behind[k])
                            )
                            if z < ZS:
                                fresh = fresh * in_before
                            if z >= 2 * ZS:
                                fresh = fresh * in_after
                            if last:
                                store(z - ZS, j, p, i, fresh * smooth_step)
                            else:
                                target[z, j, p, 8 * i : 8 * i + 8] = fresh
                if z < ZS:
                    flux_z = [f * in_before for f in flux_z]
                flux_before = flux_z
                current = above
            return carry

        lax.fori_loop(0, TILES, one_tile, 0, unroll=3)


SMOOTH_SCRATCH = [
    pltpu.VMEM((3 * ZS, TILES, 2, XW + 8, 128), F32),
    pltpu.VMEM((3 * ZS, TILES, 2, XW + 8, 128), F32),
    pltpu.VMEM((3 * ZS, XW, 128), F32),
]


def smooth_project_kernel(
    place, steps, fractions, own, before, after, state, rows_ref, rows16_ref, one, two, along
):
    def store(z, j, p, i, value):
        state[j, pl.ds(64 * i + 4 * p + z, 8, stride=8), :] = value

    smooth(
        own, before, after, (one, two), along,
        place[3].astype(F32), place[4].astype(F32), store,
    )
    project(state, steps, fractions, SUBSET, rows_ref, rows16_ref)


def smooth_end_kernel(place, own, before, after, out, one, two, along):
    def store(z, j, p, i, value):
        two[z, j, p, 8 * i : 8 * i + 8] = value

    smooth(
        own, before, after, (one, two), along,
        place[3].astype(F32), place[4].astype(F32), store,
    )
    matrix = split_matrix(True)
    column = place[0]
    for j in range(TILES - 1):
        pixels = jnp.concatenate(
            [
                jnp.concatenate([two[z, j + column, p, :XW] for p in range(2)], axis=1)
                for z in range(ZS)
            ],
            axis=0,
        )
        joined = jnp.dot(pixels, matrix, precision=HIGHEST, preferred_element_type=F32)
        out[:, :, 256 * j : 256 * j + 256] = joined.reshape(ZS, XW, 256)


def to_next(value):
    count = lax.axis_size("gz")
    return lax.ppermute(value, "gz", [(i, i + 1) for i in range(count - 1)])


def to_before(value):
    count = lax.axis_size("gz")
    return lax.ppermute(value, "gz", [(i + 1, i) for i in range(count - 1)])


def swap_halves(value):
    return lax.ppermute(value, "col", [(0, 1), (1, 0)])


def body(volume, images, owners, subsets, offsets):
    slab_count = lax.axis_size("gz")
    slab = lax.axis_index("gz")
    column = lax.axis_index("col")
    stored = images.shape[0]
    nviews = owners.shape[0]

    edge = swap_halves(jnp.where(column == 0, volume[:, :, -256:], volume[:, :, :256]))
    views = subsets.reshape(-1)
    packed = pack(0, owners, subsets, offsets, images)
    packed, edge = lax.optimization_barrier((packed, edge))
    recv = lax.all_to_all(packed, "gz", 0, 0)

    positions = jnp.sum(
        jnp.where(
            owners[None, :] == views[:, None], jnp.arange(nviews, dtype=jnp.int32)[None, :], 0
        ),
        axis=1,
    )
    owner = positions // stored
    rank = jnp.sum(
        (
            (owner[None, :] == owner[:, None]) & (positions[None, :] < positions[:, None])
        ).astype(jnp.int32),
        axis=1,
    )
    steps, fractions = view_geometry(views, XW, MARGIN, nviews)
    steps, fractions = steps.reshape(-1), fractions.reshape(-1)

    own_start = offsets[slab]
    before_start = offsets[jnp.maximum(slab - 1, 0)]
    next_start = offsets[jnp.minimum(slab + 1, slab_count - 1)]
    place = jnp.stack(
        [
            column,
            own_start - before_start,
            own_start - next_start,
            (slab > 0).astype(jnp.int32),
            (slab < slab_count - 1).astype(jnp.int32),
        ]
    ).astype(jnp.int32)

    state, rows, rows16 = scalar_call(
        start_kernel, (place, steps, fractions), (volume, edge), ROWS_OUT, [], "split_project"
    )
    later_images, recv = lax.optimization_barrier((images, recv))

    def fetch_more():
        more = lax.all_to_all(pack(2, owners, subsets, offsets, later_images), "gz", 0, 0)
        return more[owner]

    extra = lax.cond(
        jnp.max(rank) >= 2,
        fetch_more,
        lambda: jnp.zeros((views.shape[0],) + recv.shape[1:], recv.dtype),
    )
    edges = swap_halves(inner_edges(place, owner, rank, recv, extra))
    for subset in range(SUBSETS):
        fresh, low_side, high_side = update(
            subset, place, owner, rank, steps, fractions, recv, extra,
            state, rows, to_next(rows16), to_before(rows16), edges,
        )
        around = (fresh, to_next(high_side), to_before(low_side))
        if subset < SUBSETS - 1:
            state, rows, rows16 = scalar_call(
                smooth_project_kernel, (place, steps, fractions), around, ROWS_OUT,
                SMOOTH_SCRATCH, "smooth_project",
            )
    return scalar_call(
        smooth_end_kernel, (place,), around,
        jax.ShapeDtypeStruct(volume.shape, F32), SMOOTH_SCRATCH, "smooth_join",
    )


def solution(mesh):
    in_specs = (P("gz", None, "col"), P("gz", None, "col"), P(), P(), P())
    out_specs = P("gz", None, "col")
    return jax.shard_map(body, mesh=mesh, in_specs=in_specs, out_specs=out_specs, check_vma=False)
```
